256 devices in a mesh: grp: 4 (over x), dom: 64 (over y, z, core).
Axes of the slice: x: 4, y: 4, z: 8, core: 2. Of those that a mesh axis runs over, the one named last changes fastest.
Arguments:
- state: float32 [65536, 12, 128], P(('grp', 'dom'))
- neighbours: int32 [65536, 4], P(('grp', 'dom')), may hold values from 0 to 511
- pair_mask: int32 [65536, 4], P(('grp', 'dom')), may hold values from 0 to 1, as said below
- send_lists: int32 [256, 4, 64], P(('grp', 'dom')), may hold values from 0 to 255, as said below
- send_counts: int32 [256, 4], P(('grp', 'dom')), may hold values from 1 to 64, as said below
- movers: int32 [256, 64, 16], P(('grp', 'dom')), may hold values from 0 to 32767, as said below
- mover_counts: int32 [256, 64], P(('grp', 'dom')), may hold values from 0 to 16, as said below
Outputs:
- kept: float32 [65536, 12, 128], P(('grp', 'dom'))
- arrivals: float32 [12, 262144], P(None, ('grp', 'dom'))
The draws below stay inside these ranges and needn't reach their ends.
Inputs may be any that keep to these rules, and one draw needn't show every extreme that they name: `neighbours`: below 256: the device's own blocks; then 64 slots from each of lower domain, upper domain, lower slab, upper slab. `pair_mask`: 1 marks a live pair block, 0 padding. `send_lists`: each list holds distinct own block numbers. `send_counts`: on each device one of the four lists is full. `movers`: all particle numbers of a device are distinct. `mover_counts`: zero toward the device's own domain; on each device some other domain gets 16.
All inputs are finite; a program needn't handle non-finite values.
Results may differ from the reference program's by a relative error of at most 0.00007.
Values sent between devices are 32-bit elements; how exact they have to be, the bound alone decides.
A program may use at most 64 MiB of HBM per device.

```python
import jax
import jax.numpy as jnp
from jax import lax

NB = 256
K = 4
MS = 16
HB = 64
GROUPS = 4
DOMS = 64
DEVS = 256
BLOCKS = 65536
ARRIVE = 262144


def draw_state(key, part):
    keys = jax.random.split(key, 8)
    position = jax.random.uniform(keys[0], (BLOCKS, 3, 128), jnp.float32)
    velocity = jnp.clip(jax.random.normal(keys[1], (BLOCKS, 3, 128), jnp.float32), -4.0, 4.0)
    mass = jnp.exp(jax.random.uniform(keys[2], (BLOCKS, 1, 128), jnp.float32, jnp.log(0.003), jnp.log(0.03)))
    density = jax.random.uniform(keys[3], (BLOCKS, 1, 128), jnp.float32, 0.5, 2.0)
    temper = jax.random.uniform(keys[4], (BLOCKS, 1, 128), jnp.float32, 0.2, 1.2)
    solute_one = jax.random.uniform(keys[5], (BLOCKS, 1, 128), jnp.float32, 0.5, 1.5)
    solute_two = jax.random.uniform(keys[6], (BLOCKS, 1, 128), jnp.float32, 0.5, 1.5)
    solid = jax.random.uniform(keys[7], (BLOCKS, 1, 128), jnp.float32, 0.0, 0.6)
    return jnp.concatenate([position, velocity, mass, density, temper, solute_one, solute_two, solid], axis=1)


def draw_pair_mask(key, part):
    rates = jax.random.randint(jax.random.fold_in(key, 1), (DEVS, 1, 1), 1, 5)
    raw_values = jax.random.randint(jax.random.fold_in(key, 2), (DEVS, NB, K), 0, 4)
    return (raw_values < rates).astype(jnp.int32).reshape(BLOCKS, K)


def draw_send_lists(key, part):
    keys = jax.random.split(jax.random.fold_in(key, 3), DEVS * 4)
    rows_all = jax.vmap(lambda single: jax.random.permutation(single, NB)[:HB])(keys)
    return rows_all.reshape(DEVS, 4, HB).astype(jnp.int32)


def draw_send_counts(key, part):
    counts = jax.random.randint(jax.random.fold_in(key, 4), (DEVS, 4), 1, HB + 1)
    full_peer = jax.random.randint(jax.random.fold_in(key, 5), (DEVS, 1), 0, 4)
    return jnp.where(jnp.arange(4)[None, :] == full_peer, HB, counts).astype(jnp.int32)


def draw_movers(key, part):
    keys = jax.random.split(jax.random.fold_in(key, 6), DEVS)
    rows_all = jax.vmap(lambda single: jax.random.permutation(single, NB * 128)[:DOMS * MS])(keys)
    return rows_all.reshape(DEVS, DOMS, MS).astype(jnp.int32)


def draw_mover_counts(key, part):
    counts = jax.random.randint(jax.random.fold_in(key, 7), (DEVS, DOMS), 0, MS + 1)
    own_domain = (jnp.arange(DEVS) % DOMS)[:, None]
    offset = jax.random.randint(jax.random.fold_in(key, 8), (DEVS, 1), 1, DOMS)
    full_domain = (own_domain + offset) % DOMS
    column = jnp.arange(DOMS)[None, :]
    counts = jnp.where(column == full_domain, MS, counts)
    counts = jnp.where(column == own_domain, 0, counts)
    return counts.astype(jnp.int32)


def touch_ends(values, rng, low, top_value):
    shape = values.shape
    index_at = [jax.random.randint(jax.random.fold_in(rng, axis), (), 0, shape[axis]) for axis in range(len(shape))]
    values = values.at[tuple(index_at)].set(low)
    longest = shape.index(max(shape))
    index_at[longest] = (index_at[longest] + 1) % shape[longest]
    return values.at[tuple(index_at)].set(top_value)


def setup_inputs(seed: int = 0) -> dict:
    seeds = jax.random.split(jax.random.key(seed), 8)
    state = draw_state(jax.random.fold_in(seeds[7], 71), 0)
    neighbours = touch_ends(jax.random.randint(seeds[1], (BLOCKS, K), 0, NB + 4 * HB), jax.random.fold_in(seeds[1], 1), 0, (NB + 4 * HB) - 1).astype(jnp.int32)
    pair_mask = draw_pair_mask(jax.random.fold_in(seeds[7], 71), 0)
    send_lists = draw_send_lists(jax.random.fold_in(seeds[7], 71), 0)
    send_counts = draw_send_counts(jax.random.fold_in(seeds[7], 71), 0)
    movers = draw_movers(jax.random.fold_in(seeds[7], 71), 0)
    mover_counts = draw_mover_counts(jax.random.fold_in(seeds[7], 71), 0)
    return dict(state=state, neighbours=neighbours, pair_mask=pair_mask, send_lists=send_lists, send_counts=send_counts, movers=movers, mover_counts=mover_counts)


def payload(state):
    mass = state[:, 6]
    volume = mass / state[:, 7]
    return jnp.concatenate([state[:, 0:3], mass[:, None], volume[:, None], state[:, 8:11], state[:, 3:6]], axis=1)


def block_tile_sums(owned_here, nearby_particles, alive_flags):
    radius = jnp.zeros((owned_here.shape[0], 128, 128), jnp.float32)
    for comp in range(3):
        delta = owned_here[:, comp, :, None] - nearby_particles[:, comp, None, :]
        radius = radius + delta * delta
    smoothing_kernel = jnp.maximum(0.0, 1.0 - 2.0 * radius)
    kernel_weight = smoothing_kernel * smoothing_kernel * smoothing_kernel * alive_flags[:, None, None]
    volume = nearby_particles[:, 4]
    carried = jnp.concatenate([nearby_particles[:, 3:5], volume[:, None] * nearby_particles[:, 5:11]], axis=1)
    return jnp.einsum("gij,gcj->gci", kernel_weight, carried, precision=lax.Precision.HIGHEST)


def advance(state, sums):
    position = state[:, 0:3]
    velocity = state[:, 3:6]
    temper = state[:, 8]
    solute_one = state[:, 9]
    solute_two = state[:, 10]
    solid = state[:, 11]
    sum_volume = sums[:, 1]
    temp_one = temper + 0.25 * (sums[:, 2] - temper * sum_volume)
    conc_one = solute_one + 0.2 * (sums[:, 3] - solute_one * sum_volume)
    conc_two = solute_two + 0.1 * (sums[:, 4] - solute_two * sum_volume)
    velocity_new = velocity + 0.3 * (sums[:, 5:8] - velocity * sum_volume[:, None])
    position_new = position + 0.02 * velocity_new
    liquidus = 1.0 - 0.3 * conc_one - 0.2 * conc_two
    solid_new = jnp.maximum(solid, jnp.clip(2.0 * (liquidus - temp_one), 0.0, 1.0))
    temp_two = temp_one + 0.4 * (solid_new - solid)
    solute_first_updated = conc_one * (1.0 - 0.83 * solid) / (1.0 - 0.83 * solid_new)
    conc_two_new = conc_two * (1.0 - 0.6 * solid) / (1.0 - 0.6 * solid_new)
    return jnp.concatenate([position_new, velocity_new, state[:, 6:7], sums[:, 0:1], temp_two[:, None], solute_first_updated[:, None], conc_two_new[:, None], solid_new[:, None]], axis=1)


def reference(state, neighbours, pair_mask, send_lists, send_counts, movers, mover_counts):
    devices = GROUPS * DOMS
    per_dev = state.reshape(devices, NB, 12, 128)
    own = jax.vmap(payload)(per_dev)
    outgoing = jax.vmap(lambda blocks_here, chosen: blocks_here[chosen])(own, send_lists)
    filled = (jnp.arange(HB, dtype=jnp.int32)[None, None, :] < send_counts[:, :, None]).astype(jnp.float32)
    outgoing = outgoing * filled[..., None, None]
    grid = outgoing.reshape(GROUPS, DOMS, 4, HB, 11, 128)
    zero_dom = jnp.zeros((GROUPS, 1, HB, 11, 128), jnp.float32)
    zero_grp = jnp.zeros((1, DOMS, HB, 11, 128), jnp.float32)
    from_dlow = jnp.concatenate([zero_dom, grid[:, :-1, 1]], axis=1).reshape(devices, HB, 11, 128)
    from_dhigh = jnp.concatenate([grid[:, 1:, 0], zero_dom], axis=1).reshape(devices, HB, 11, 128)
    from_glow = jnp.concatenate([zero_grp, grid[:-1, :, 3]], axis=0).reshape(devices, HB, 11, 128)
    from_ghigh = jnp.concatenate([grid[1:, :, 2], zero_grp], axis=0).reshape(devices, HB, 11, 128)
    nbr_all = neighbours.reshape(devices, NB * K)
    live_all = pair_mask.reshape(devices, NB * K).astype(jnp.float32)

    def per_device(items):
        own_dev, first, second, third, fourth, nbr_dev, live_dev, state_dev = items
        candidates = jnp.concatenate([own_dev, first, second, third, fourth], axis=0)
        nearby_particles = candidates[nbr_dev]
        owned_here = jnp.repeat(own_dev, K, axis=0)
        sums = block_tile_sums(owned_here, nearby_particles, live_dev).reshape(NB, K, 8, 128).sum(axis=1)
        return advance(state_dev, sums)

    updated = lax.map(per_device, (own, from_dlow, from_dhigh, from_glow, from_ghigh, nbr_all, live_all, per_dev))
    flat = updated.transpose(0, 2, 1, 3).reshape(devices, 12, NB * 128)
    picked = movers.reshape(devices, DOMS * MS)
    sending = (jnp.arange(MS, dtype=jnp.int32)[None, None, :] < mover_counts[:, :, None]).astype(jnp.float32).reshape(devices, DOMS * MS)
    outbound = jax.vmap(lambda rows_here, chosen: rows_here[:, chosen])(flat, picked) * sending[:, None, :]
    departed = jax.vmap(lambda chosen, flags: jnp.zeros((NB * 128,), jnp.float32).at[chosen].max(flags))(picked, sending)
    kept = (flat * (1.0 - departed)[:, None, :]).reshape(devices, 12, NB, 128).transpose(0, 2, 1, 3).reshape(BLOCKS, 12, 128)
    arrivals = outbound.reshape(GROUPS, DOMS, 12, DOMS, MS).transpose(2, 0, 3, 1, 4).reshape(12, ARRIVE)
    return kept, arrivals
```

```python
import functools

import jax
import jax.numpy as jnp
from jax import lax
from jax.experimental import pallas as pl
from jax.experimental.pallas import tpu as pltpu
from jax.sharding import PartitionSpec as P

MESH = pl.DeviceIdType.MESH
F32 = jnp.float32
BF16 = jnp.bfloat16
NB = 256
HB = 64
NC = 512
FR = 48
CR = 32
U = 8
REACH = 2.0
NT = (((1,), (1,)), ((), ()))
TN = (((0,), (0,)), ((), ()))
VMEM_LIMIT = 58 << 20


def carried_planes(st, rows):
    mass = st[6, rows, :]
    volume = mass / st[7, rows, :]
    out = [mass, volume]
    for ch in (8, 9, 10, 3, 4, 5):
        out.append(volume * st[ch, rows, :])
    return out


def exchange_kernel(lists, counts, st, halo_c, halo_x, tab_c, tab_x, send_c, pick_x, send_x, ssem, rsem):
    grp, dom = lax.axis_index("grp"), lax.axis_index("dom")
    n_grp, n_dom = lax.axis_size("grp"), lax.axis_size("dom")
    has = [dom > 0, dom < n_dom - 1, grp > 0, grp < n_grp - 1]
    peer = [(grp, dom - 1), (grp, dom + 1), (grp - 1, dom), (grp + 1, dom)]
    barrier = pltpu.get_barrier_semaphore()
    for p in range(4):

        @pl.when(has[p])
        def _(p=p):
            pl.semaphore_signal(barrier, inc=1, device_id=peer[p], device_id_type=MESH)

    def build(q, carry):
        rows = pl.ds(pl.multiple_of(q * 32, 32), 32)
        for c, plane in enumerate(carried_planes(st, rows)):
            tab_c[rows, c, :] = plane
        for c in range(3):
            tab_x[rows, c, :] = st[c, rows, :]
        return carry

    lax.fori_loop(0, NB // 32, build, 0)

    def copies(p):
        slot = p ^ 1
        return [
            pltpu.make_async_remote_copy(
                src_ref=send_c.at[pl.ds(p * HB * 8, HB * 8)],
                dst_ref=halo_c.at[pl.ds(slot * HB * 8, HB * 8)],
                send_sem=ssem.at[p, 0],
                recv_sem=rsem.at[slot, 0],
                device_id=peer[p],
                device_id_type=MESH,
            ),
            pltpu.make_async_remote_copy(
                src_ref=send_x.at[:, p],
                dst_ref=halo_x.at[:, slot],
                send_sem=ssem.at[p, 1],
                recv_sem=rsem.at[slot, 1],
                device_id=peer[p],
                device_id_type=MESH,
            ),
        ]

    met = False
    for p in (3, 2, 1, 0):

        def pick(t, carry, p=p):
            for u in range(8):
                s = t * 8 + u
                live = jnp.where(s < counts[0, p], 1.0, 0.0).astype(F32)
                b = lists[p, s]
                send_c[pl.ds(pl.multiple_of(p * HB * 8 + s * 8, 8), 8), :] = tab_c[b] * live
                pick_x[pl.ds(pl.multiple_of(s * 8, 8), 8), :] = tab_x[b] * live
            return carry

        lax.fori_loop(0, HB // 8, pick, 0)
        for c in range(3):
            send_x[c, p] = pick_x[pl.ds(c, HB, stride=8), :]
        if not met:
            pl.semaphore_wait(barrier, sum(h.astype(jnp.int32) for h in has))
            met = True

        @pl.when(has[p])
        def _(p=p):
            for copy in copies(p):
                copy.start()

    for p in range(4):

        @pl.when(jnp.logical_not(has[p]))
        def _(p=p):
            halo_c[pl.ds(p * HB * 8, HB * 8), :] = jnp.zeros((HB * 8, 128), F32)
            halo_x[:, p] = jnp.zeros((3, HB, 128), F32)

    for p in range(4):

        @pl.when(has[p])
        def _(p=p):
            for copy in copies(p):
                copy.wait_send()
            for copy in copies(p ^ 1):
                copy.wait_recv()


def exchange(lists, counts, planes):
    return pl.pallas_call(
        exchange_kernel,
        out_shape=(
            jax.ShapeDtypeStruct((4 * HB * 8, 128), F32),
            jax.ShapeDtypeStruct((3, 4, HB, 128), F32),
        ),
        in_specs=[
            pl.BlockSpec(memory_space=pltpu.SMEM),
            pl.BlockSpec(memory_space=pltpu.SMEM),
            pl.BlockSpec(memory_space=pltpu.VMEM),
        ],
        out_specs=(pl.BlockSpec(memory_space=pltpu.VMEM), pl.BlockSpec(memory_space=pltpu.VMEM)),
        scratch_shapes=[
            pltpu.VMEM((NB, 8, 128), F32),
            pltpu.VMEM((NB, 8, 128), F32),
            pltpu.VMEM((4 * HB * 8, 128), F32),
            pltpu.VMEM((HB * 8, 128), F32),
            pltpu.VMEM((3, 4, HB, 128), F32),
            pltpu.SemaphoreType.DMA((4, 2)),
            pltpu.SemaphoreType.DMA((4, 2)),
        ],
        compiler_params=pltpu.CompilerParams(
            collective_id=0, has_side_effects=True, vmem_limit_bytes=VMEM_LIMIT
        ),
    )(lists, counts, planes)


def swap_groups(v):
    row = lax.broadcasted_iota(jnp.int32, (8, 128), 0)
    group = lax.broadcasted_iota(jnp.int32, (8, 128), 1) // 16
    apart = (row - group) & 7
    out = v
    for d in range(1, 8):
        moved = pltpu.roll(pltpu.roll(v, d, 0), 128 - 16 * d, 1)
        out = jnp.where(apart == d, moved, out)
    return out


def pieces(v):
    first = v.astype(BF16).astype(F32)
    rest = v - first
    second = rest.astype(BF16).astype(F32)
    return first, second, rest - second


def local_kernel(
    nbr, mask, movers_s, counts_s, st, halo_c, halo_x, movers_v, counts_v, kept, message,
    tab_x, tab_p, tab_c, feat, own_feat, car, sums, upd, *stages,
):
    dist, high, low = stages[:U], stages[U : 2 * U], stages[2 * U :]
    centre, wide = [], None
    for c in range(3):
        plane = st[c]
        top, bottom = jnp.max(plane), jnp.min(plane)
        centre.append(0.5 * top + 0.5 * bottom)
        half = 0.5 * top - 0.5 * bottom
        wide = half if wide is None else jnp.maximum(wide, half)
    close = wide <= REACH

    def features(q, carry):
        own = pl.ds(pl.multiple_of(q * 32, 32), 32)
        zero, one = jnp.zeros((32, 128), F32), jnp.ones((32, 128), F32)
        for first in (0, NB):
            norm, xs = None, []
            for c in range(3):
                raw = st[c, own, :] if first == 0 else halo_x[c, own, :]
                x = jnp.clip(raw - centre[c], -REACH - 1.0, REACH + 1.0)
                norm = x * x if norm is None else norm + x * x
                xs.append(x)
            for c, plane in enumerate([*xs, 0.5 - norm, one, zero, zero, zero]):
                tab_x[pl.ds(first * 8 + q * 256 + c, 32, stride=8), :] = plane
            if first == 0:
                for c, plane in enumerate([*[2.0 * x for x in xs], one, -norm, zero, zero, zero]):
                    tab_p[pl.ds(q * 256 + c, 32, stride=8), :] = plane
        for c, plane in enumerate(carried_planes(st, own)):
            tab_c[pl.ds(q * 256 + c, 32, stride=8), :] = plane
        return carry

    lax.fori_loop(0, NB // 32, features, 0)

    def convert(q, carry):
        for u in range(8):
            b = q * 8 + u
            at = pl.ds(pl.multiple_of(b * 8, 8), 8)
            for n, own in ((b, True), (b + NB, False)):
                x1, x2, x3 = pieces(tab_x[pl.ds(pl.multiple_of(n * 8, 8), 8), :])
                feat[n] = jnp.concatenate([x1, x2, x3, x1, x2, x1], 0).astype(BF16)
                c1, c2, c3 = pieces(tab_c[at, :] if own else halo_c[at, :])
                car[n] = jnp.concatenate([c1, c2, c3, jnp.zeros_like(c1)], 0).astype(BF16)
            p1, p2, p3 = pieces(tab_p[at, :])
            own_feat[b] = jnp.concatenate([p1, p1, p1, p2, p2, p3], 0).astype(BF16)
        return carry

    lax.fori_loop(0, NB // 8, convert, 0)
    feat[NC] = jnp.zeros((FR, 128), BF16)
    car[NC] = jnp.zeros((CR, 128), BF16)

    def slot(k, i):
        return jnp.where(mask[k, i] == 0, NC, nbr[k, i])

    def store_sums(i, r):
        sums[pl.ds(pl.multiple_of(i * 8, 8), 8), :] = r[0:8] + r[8:16] + r[16:24]

    def split(w):
        h = w.astype(BF16)
        return h, (w - h.astype(F32)).astype(BF16)

    def measure(i, u):
        for half in range(2):
            near = jnp.concatenate([feat[slot(2 * half + k, i)] for k in range(2)], 1)
            dist[u][:, half * 256 : half * 256 + 256] = lax.dot_general(
                own_feat[i], near, TN, preferred_element_type=F32
            )

    def weigh(u):
        for half in range(2):
            cols = slice(half * 256, half * 256 + 256)
            s = jnp.maximum(dist[u][:, cols], 0.0)
            h, rest = split(s * s * s)
            high[u][:, cols] = h
            low[u][:, cols] = rest

    def contract(i, u):
        c = jnp.concatenate([car[slot(k, i)] for k in range(4)], 1)
        r = lax.dot_general(c, high[u][...], NT, preferred_element_type=F32)
        r = r + lax.dot_general(c, low[u][...], NT, preferred_element_type=F32)
        store_sums(i, r)

    @pl.when(close)
    def _():
        def body(t, carry):
            for u in range(U):
                i = t * U + u
                contract(jnp.maximum(i - 2, 0), (u - 2) % U)
                weigh((u - 1) % U)
                measure(i, u)
            return carry

        lax.fori_loop(0, NB // U, body, 0)
        contract(NB - 2, U - 2)
        weigh(U - 1)
        contract(NB - 1, U - 1)

    @pl.when(jnp.logical_not(close))
    def _():
        def raw(q, carry):
            own = pl.ds(pl.multiple_of(q * 32, 32), 32)
            for c in range(3):
                tab_x[pl.ds(q * 256 + c, 32, stride=8), :] = st[c, own, :]
                tab_x[pl.ds(NB * 8 + q * 256 + c, 32, stride=8), :] = halo_x[c, own, :]
            return carry

        lax.fori_loop(0, NB // 32, raw, 0)

        def body(i, carry):
            columns = jnp.transpose(tab_x[pl.ds(pl.multiple_of(i * 8, 8), 8), :])

            def pair(k, total):
                near = tab_x[pl.ds(pl.multiple_of(nbr[k, i] * 8, 8), 8), :]
                s = jnp.full((128, 128), 0.5, F32)
                for c in range(3):
                    delta = columns[:, c : c + 1] - near[c : c + 1, :]
                    s = s - delta * delta
                s = jnp.maximum(s, 0.0)
                h, rest = split(s * s * s)
                cc = car[slot(k, i)]
                r = lax.dot_general(cc, h, NT, preferred_element_type=F32)
                return total + r + lax.dot_general(cc, rest, NT, preferred_element_type=F32)

            store_sums(i, lax.fori_loop(0, 4, pair, jnp.zeros((CR, 128), F32)))
            return carry

        lax.fori_loop(0, NB, body, 0)

    mv = movers_v[...]
    per = mv.shape[0]
    slot_of = lax.broadcasted_iota(jnp.int32, mv.shape, 0)
    live = slot_of < counts_v[...]
    block_of = jnp.where(live, mv // 128, -1)
    lane_of = mv % 128
    gone = jnp.zeros((NB, 128), F32)
    for r in range(0, per, 2):
        b = jnp.concatenate([block_of[r : r + 1], block_of[r + 1 : r + 2]], 1)
        ln = jnp.concatenate([lane_of[r : r + 1], lane_of[r + 1 : r + 2]], 1)
        in_block = (lax.broadcasted_iota(jnp.int32, (NB, 128), 0) == b).astype(F32).astype(BF16)
        in_lane = (lax.broadcasted_iota(jnp.int32, (128, 128), 0) == ln).astype(F32).astype(BF16)
        gone = gone + lax.dot_general(in_block, in_lane, NT, preferred_element_type=F32)
    kept[0] = 1.0 - gone

    def advance(q, carry):
        rows = pl.ds(pl.multiple_of(q * 32, 32), 32)
        total = [8.0 * sums[pl.ds(q * 256 + c, 32, stride=8), :] for c in range(8)]
        position = [st[c, rows, :] for c in range(3)]
        velocity = [st[3 + c, rows, :] for c in range(3)]
        temper, one, two, solid = (st[c, rows, :] for c in range(8, 12))
        vol = total[1]
        temp_one = temper + 0.25 * (total[2] - temper * vol)
        conc_one = one + 0.2 * (total[3] - one * vol)
        conc_two = two + 0.1 * (total[4] - two * vol)
        v_new = [velocity[c] + 0.3 * (total[5 + c] - velocity[c] * vol) for c in range(3)]
        x_new = [position[c] + 0.02 * v_new[c] for c in range(3)]
        liquidus = 1.0 - 0.3 * conc_one - 0.2 * conc_two
        solid_new = jnp.maximum(solid, jnp.clip(2.0 * (liquidus - temp_one), 0.0, 1.0))
        temp_two = temp_one + 0.4 * (solid_new - solid)
        one_new = conc_one * (1.0 - 0.83 * solid) / (1.0 - 0.83 * solid_new)
        two_new = conc_two * (1.0 - 0.6 * solid) / (1.0 - 0.6 * solid_new)
        updated = [*x_new, *v_new, st[6, rows, :], total[0], temp_two, one_new, two_new, solid_new]
        stay = kept[0, rows, :]
        for c, plane in enumerate(updated):
            kept[c, rows, :] = plane * stay
            upd[pl.ds(q * 512 + c, 32, stride=16), :] = plane
        zero = jnp.zeros((32, 128), F32)
        for c in range(12, 16):
            upd[pl.ds(q * 512 + c, 32, stride=16), :] = zero
        return carry

    lax.fori_loop(0, NB // 32, advance, 0)

    upd[pl.ds(NB * 16, 16), :] = jnp.zeros((16, 128), F32)
    lane = lax.broadcasted_iota(jnp.int32, (16, 128), 1)

    def gather(g, carry):
        acc = jnp.zeros((16, 128), F32)
        for t in range(128):
            m = movers_s[t % 16, g * 8 + t // 16]
            b, ln = lax.shift_right_logical(m, 7), m & 127
            b = jnp.where(t % 16 < counts_s[0, g * 8 + t // 16], b, NB)
            v = upd[pl.ds(pl.multiple_of(b * 16, 16), 16), :]
            acc = jnp.where(lane == t, pltpu.roll(v, (t - ln) & 127, 1), acc)
        for h in range(2):
            message[pl.ds(g * 16 + h, 8, stride=2), :] = swap_groups(acc[8 * h : 8 * h + 8])
        return carry

    lax.fori_loop(0, movers_s.shape[1] // 8, gather, 0)


def local_step(nbr, mask, movers, planes, halo_c, halo_x, counts):
    smem, vmem = pl.BlockSpec(memory_space=pltpu.SMEM), pl.BlockSpec(memory_space=pltpu.VMEM)
    doms = movers.shape[1]
    return pl.pallas_call(
        local_kernel,
        out_shape=(
            jax.ShapeDtypeStruct((12, NB, 128), F32),
            jax.ShapeDtypeStruct((2 * doms, 128), F32),
        ),
        in_specs=[smem, smem, smem, smem, vmem, vmem, vmem, vmem, vmem],
        out_specs=(vmem, vmem),
        scratch_shapes=[
            pltpu.VMEM((NC * 8, 128), F32),
            pltpu.VMEM((NB * 8, 128), F32),
            pltpu.VMEM((NB * 8, 128), F32),
            pltpu.VMEM((NC + 1, FR, 128), BF16),
            pltpu.VMEM((NB, FR, 128), BF16),
            pltpu.VMEM((NC + 1, CR, 128), BF16),
            pltpu.VMEM((NB * 8, 128), F32),
            pltpu.VMEM((NB * 16 + 16, 128), F32),
            *[pltpu.VMEM((128, 512), F32)] * U,
            *[pltpu.VMEM((128, 512), BF16)] * (2 * U),
        ],
        compiler_params=pltpu.CompilerParams(vmem_limit_bytes=VMEM_LIMIT),
    )(nbr, mask, movers, counts, planes, halo_c, halo_x, movers, counts)


def migrate_kernel(doms, message, out, landed, ssem, rsem):
    grp, me = lax.axis_index("grp"), lax.axis_index("dom")
    barrier = pltpu.get_barrier_semaphore()

    def greet(k, carry):
        other = lax.rem(me + k, doms)
        pl.semaphore_signal(barrier, inc=1, device_id=(grp, other), device_id_type=MESH)
        return carry

    lax.fori_loop(1, doms, greet, 0)
    landed[me] = message[me]
    pl.semaphore_wait(barrier, doms - 1)

    def copy(k):
        other = lax.rem(me + k, doms)
        return pltpu.make_async_remote_copy(
            src_ref=message.at[other],
            dst_ref=landed.at[me],
            send_sem=ssem.at[k],
            recv_sem=rsem.at[k],
            device_id=(grp, other),
            device_id_type=MESH,
        )

    def send(k, carry):
        copy(k).start()
        return carry

    def finish(k, carry):
        copy(k).wait()
        return carry

    lax.fori_loop(1, doms, send, 0)
    lax.fori_loop(1, doms, finish, 0)
    for g in range(doms // 8):
        cols = slice(g * 128, g * 128 + 128)
        for h in range(2):
            rows = 8 if h == 0 else 4
            v = swap_groups(landed[pl.ds(g * 8, 8), h, :])
            out[8 * h : 8 * h + rows, cols] = v[:rows]


def migrate(message):
    doms = message.shape[0]
    vmem = pl.BlockSpec(memory_space=pltpu.VMEM)
    return pl.pallas_call(
        functools.partial(migrate_kernel, doms),
        out_shape=jax.ShapeDtypeStruct((12, doms * 16), F32),
        in_specs=[vmem],
        out_specs=vmem,
        scratch_shapes=[
            pltpu.VMEM((doms, 2, 128), F32),
            pltpu.SemaphoreType.DMA((doms,)),
            pltpu.SemaphoreType.DMA((doms,)),
        ],
        compiler_params=pltpu.CompilerParams(collective_id=1, has_side_effects=True),
    )(message)


def on_device(state, neighbours, pair_mask, send_lists, send_counts, movers, mover_counts):
    planes = state.transpose(1, 0, 2)
    halo_c, halo_x = exchange(send_lists[0], send_counts, planes)
    kept, message = local_step(
        neighbours.T, pair_mask.T, movers[0].T, planes, halo_c, halo_x.reshape(3, 4 * HB, 128), mover_counts
    )
    arrivals = migrate(message.reshape(-1, 2, 128))
    return kept.transpose(1, 0, 2), arrivals


def solution(mesh):
    both = ("grp", "dom")
    placed = (P(both, None, None), P(both, None), P(both, None), P(both, None, None), P(both, None), P(both, None, None), P(both, None))
    return jax.shard_map(
        on_device,
        mesh=mesh,
        in_specs=placed,
        out_specs=(P(both, None, None), P(None, both)),
        check_vma=False,
    )
```

```python
import jax
import jax.numpy as jnp
from jax import lax
from jax.experimental import pallas as pl
from jax.experimental.pallas import tpu as pltpu
from jax.sharding import PartitionSpec as P

MESH = pl.DeviceIdType.MESH
F32 = jnp.float32
BF16 = jnp.bfloat16
NB = 256
HB = 64
NC = 512
FR = 48
CR = 32
U = 8
REACH = 2.0
NT = (((1,), (1,)), ((), ()))
TN = (((0,), (0,)), ((), ()))
VMEM_LIMIT = 40 << 20


def carried_planes(st, rows):
    mass = st[6, rows, :]
    volume = mass / st[7, rows, :]
    out = [mass, volume]
    for ch in (8, 9, 10, 3, 4, 5):
        out.append(volume * st[ch, rows, :])
    return out


def pieces(v):
    first = v.astype(BF16).astype(F32)
    rest = v - first
    second = rest.astype(BF16).astype(F32)
    return first, second, rest - second


def exchange_kernel(
    lists, counts, st, movers, mover_counts, halo_x, feat, own_feat, car, stay,
    halo_c, tab_c, tab_x, near_x, tab_p, send_c, pick_x, send_x, ssem, rsem,
):
    grp, dom = lax.axis_index("grp"), lax.axis_index("dom")
    n_grp, n_dom = lax.axis_size("grp"), lax.axis_size("dom")
    has = [dom > 0, dom < n_dom - 1, grp > 0, grp < n_grp - 1]
    peer = [(grp, dom - 1), (grp, dom + 1), (grp - 1, dom), (grp + 1, dom)]
    barrier = pltpu.get_barrier_semaphore()
    for p in range(4):

        @pl.when(has[p])
        def _(p=p):
            pl.semaphore_signal(barrier, inc=1, device_id=peer[p], device_id_type=MESH)

    def build(q, carry):
        rows = pl.ds(pl.multiple_of(q * 32, 32), 32)
        for c, plane in enumerate(carried_planes(st, rows)):
            tab_c[rows, c, :] = plane
        for c in range(3):
            tab_x[rows, c, :] = st[c, rows, :]
        return carry

    lax.fori_loop(0, NB // 32, build, 0)

    def copies(p):
        slot = p ^ 1
        return [
            pltpu.make_async_remote_copy(
                src_ref=send_c.at[pl.ds(p * HB * 8, HB * 8)],
                dst_ref=halo_c.at[pl.ds(slot * HB * 8, HB * 8)],
                send_sem=ssem.at[p, 0],
                recv_sem=rsem.at[slot, 0],
                device_id=peer[p],
                device_id_type=MESH,
            ),
            pltpu.make_async_remote_copy(
                src_ref=send_x.at[:, p],
                dst_ref=halo_x.at[:, pl.ds(slot * HB, HB)],
                send_sem=ssem.at[p, 1],
                recv_sem=rsem.at[slot, 1],
                device_id=peer[p],
                device_id_type=MESH,
            ),
        ]

    met = False
    for p in (3, 2, 1, 0):

        def pick(t, carry, p=p):
            for u in range(8):
                s = t * 8 + u
                live = jnp.where(s < counts[0, p], 1.0, 0.0).astype(F32)
                b = lists[p, s]
                send_c[pl.ds(pl.multiple_of(p * HB * 8 + s * 8, 8), 8), :] = tab_c[b] * live
                pick_x[pl.ds(pl.multiple_of(s * 8, 8), 8), :] = tab_x[b] * live
            return carry

        lax.fori_loop(0, HB // 8, pick, 0)
        for c in range(3):
            send_x[c, p] = pick_x[pl.ds(c, HB, stride=8), :]
        if not met:
            pl.semaphore_wait(barrier, sum(h.astype(jnp.int32) for h in has))
            met = True

        @pl.when(has[p])
        def _(p=p):
            for copy in copies(p):
                copy.start()

    for p in range(4):

        @pl.when(jnp.logical_not(has[p]))
        def _(p=p):
            halo_c[pl.ds(p * HB * 8, HB * 8), :] = jnp.zeros((HB * 8, 128), F32)
            halo_x[:, pl.ds(p * HB, HB), :] = jnp.zeros((3, HB, 128), F32)

    centre = [0.5 * jnp.max(st[c]) + 0.5 * jnp.min(st[c]) for c in range(3)]

    def features(source, own):
        def body(q, carry):
            rows = pl.ds(pl.multiple_of(q * 32, 32), 32)
            zero, one = jnp.zeros((32, 128), F32), jnp.ones((32, 128), F32)
            norm, xs = None, []
            for c in range(3):
                x = jnp.clip(source[c, rows, :] - centre[c], -REACH - 1.0, REACH + 1.0)
                norm = x * x if norm is None else norm + x * x
                xs.append(x)
            for c, plane in enumerate([*xs, 0.5 - norm, one, zero, zero, zero]):
                near_x[pl.ds(q * 256 + c, 32, stride=8), :] = plane
            if own:
                for c, plane in enumerate([*[2.0 * x for x in xs], one, -norm, zero, zero, zero]):
                    tab_p[pl.ds(q * 256 + c, 32, stride=8), :] = plane
            return carry

        lax.fori_loop(0, NB // 32, body, 0)

    def convert(own):
        def body(q, carry):
            for u in range(8):
                b = q * 8 + u
                at = pl.ds(pl.multiple_of(b * 8, 8), 8)
                n = b if own else b + NB
                x1, x2, x3 = pieces(near_x[at, :])
                feat[n] = jnp.concatenate([x1, x2, x3, x1, x2, x1], 0).astype(BF16)
                c1, c2, c3 = pieces(tab_c[b] if own else halo_c[at, :])
                car[n] = jnp.concatenate([c1, c2, c3, jnp.zeros_like(c1)], 0).astype(BF16)
                if own:
                    p1, p2, p3 = pieces(tab_p[at, :])
                    own_feat[b] = jnp.concatenate([p1, p1, p1, p2, p2, p3], 0).astype(BF16)
            return carry

        lax.fori_loop(0, NB // 8, body, 0)

    features(st, True)
    convert(True)
    feat[NC] = jnp.zeros((FR, 128), BF16)
    car[NC] = jnp.zeros((CR, 128), BF16)

    mv = movers[...]
    per = mv.shape[0]
    live = lax.broadcasted_iota(jnp.int32, mv.shape, 0) < mover_counts[...]
    block_of = jnp.where(live, lax.shift_right_logical(mv, 7), -1)
    lane_of = mv & 127
    gone = jnp.zeros((NB, 128), F32)
    for r in range(0, per, 2):
        b = jnp.concatenate([block_of[r : r + 1], block_of[r + 1 : r + 2]], 1)
        ln = jnp.concatenate([lane_of[r : r + 1], lane_of[r + 1 : r + 2]], 1)
        in_block = (lax.broadcasted_iota(jnp.int32, (NB, 128), 0) == b).astype(F32).astype(BF16)
        in_lane = (lax.broadcasted_iota(jnp.int32, (128, 128), 0) == ln).astype(F32).astype(BF16)
        gone = gone + lax.dot_general(in_block, in_lane, NT, preferred_element_type=F32)
    stay[...] = 1.0 - gone

    for p in range(4):

        @pl.when(has[p])
        def _(p=p):
            for copy in copies(p):
                copy.wait_send()
            for copy in copies(p ^ 1):
                copy.wait_recv()

    features(halo_x, False)
    convert(False)


def exchange(lists, counts, planes, movers, mover_counts):
    smem, vmem = pl.BlockSpec(memory_space=pltpu.SMEM), pl.BlockSpec(memory_space=pltpu.VMEM)
    return pl.pallas_call(
        exchange_kernel,
        out_shape=(
            pltpu.VMEM((3, 4 * HB, 128), F32),
            pltpu.VMEM((NC + 1, FR, 128), BF16),
            pltpu.VMEM((NB, FR, 128), BF16),
            pltpu.VMEM((NC + 1, CR, 128), BF16),
            pltpu.VMEM((NB, 128), F32),
        ),
        in_specs=[smem, smem, vmem, vmem, vmem],
        out_specs=(vmem,) * 5,
        scratch_shapes=[
            pltpu.VMEM((4 * HB * 8, 128), F32),
            pltpu.VMEM((NB, 8, 128), F32),
            pltpu.VMEM((NB, 8, 128), F32),
            pltpu.VMEM((NB * 8, 128), F32),
            pltpu.VMEM((NB * 8, 128), F32),
            pltpu.VMEM((4 * HB * 8, 128), F32),
            pltpu.VMEM((HB * 8, 128), F32),
            pltpu.VMEM((3, 4, HB, 128), F32),
            pltpu.SemaphoreType.DMA((4, 2)),
            pltpu.SemaphoreType.DMA((4, 2)),
        ],
        compiler_params=pltpu.CompilerParams(
            collective_id=0, has_side_effects=True, vmem_limit_bytes=VMEM_LIMIT
        ),
    )(lists, counts, planes, movers, mover_counts)


def swap_groups(v):
    row = lax.broadcasted_iota(jnp.int32, (8, 128), 0)
    group = lax.broadcasted_iota(jnp.int32, (8, 128), 1) // 16
    apart = (row - group) & 7
    out = v
    for d in range(1, 8):
        moved = pltpu.roll(pltpu.roll(v, d, 0), 128 - 16 * d, 1)
        out = jnp.where(apart == d, moved, out)
    return out


def local_kernel(
    nbr, mask, movers_s, counts_s, st, halo_x, feat, own_feat, car, stay_ref, kept, message,
    tab_x, sums, upd, *stages,
):
    dist, high, low = stages[:U], stages[U : 2 * U], stages[2 * U :]
    wide = None
    for c in range(3):
        half = 0.5 * jnp.max(st[c]) - 0.5 * jnp.min(st[c])
        wide = half if wide is None else jnp.maximum(wide, half)
    close = wide <= REACH

    def slot(k, i):
        return jnp.where(mask[k, i] == 0, NC, nbr[k, i])

    def store_sums(i, r):
        sums[pl.ds(pl.multiple_of(i * 8, 8), 8), :] = r[0:8] + r[8:16] + r[16:24]

    def split(w):
        h = w.astype(BF16)
        return h, (w - h.astype(F32)).astype(BF16)

    def measure(i, u):
        for half in range(2):
            near = jnp.concatenate([feat[slot(2 * half + k, i)] for k in range(2)], 1)
            dist[u][:, half * 256 : half * 256 + 256] = lax.dot_general(
                own_feat[i], near, TN, preferred_element_type=F32
            )

    def weigh(u):
        for half in range(2):
            cols = slice(half * 256, half * 256 + 256)
            s = jnp.maximum(dist[u][:, cols], 0.0)
            h, rest = split(s * s * s)
            high[u][:, cols] = h
            low[u][:, cols] = rest

    def contract(i, u):
        c = jnp.concatenate([car[slot(k, i)] for k in range(4)], 1)
        r = lax.dot_general(c, high[u][...], NT, preferred_element_type=F32)
        r = r + lax.dot_general(c, low[u][...], NT, preferred_element_type=F32)
        store_sums(i, r)

    @pl.when(close)
    def _():
        def body(t, carry):
            for u in range(U):
                i = t * U + u
                contract(jnp.maximum(i - 2, 0), (u - 2) % U)
                weigh((u - 1) % U)
                measure(i, u)
            return carry

        lax.fori_loop(0, NB // U, body, 0)
        contract(NB - 2, U - 2)
        weigh(U - 1)
        contract(NB - 1, U - 1)

    @pl.when(jnp.logical_not(close))
    def _():
        def raw(q, carry):
            own = pl.ds(pl.multiple_of(q * 32, 32), 32)
            for c in range(3):
                tab_x[pl.ds(q * 256 + c, 32, stride=8), :] = st[c, own, :]
                tab_x[pl.ds(NB * 8 + q * 256 + c, 32, stride=8), :] = halo_x[c, own, :]
            return carry

        lax.fori_loop(0, NB // 32, raw, 0)

        def body(i, carry):
            columns = jnp.transpose(tab_x[pl.ds(pl.multiple_of(i * 8, 8), 8), :])

            def pair(k, total):
                near = tab_x[pl.ds(pl.multiple_of(nbr[k, i] * 8, 8), 8), :]
                s = jnp.full((128, 128), 0.5, F32)
                for c in range(3):
                    delta = columns[:, c : c + 1] - near[c : c + 1, :]
                    s = s - delta * delta
                s = jnp.maximum(s, 0.0)
                h, rest = split(s * s * s)
                cc = car[slot(k, i)]
                r = lax.dot_general(cc, h, NT, preferred_element_type=F32)
                return total + r + lax.dot_general(cc, rest, NT, preferred_element_type=F32)

            store_sums(i, lax.fori_loop(0, 4, pair, jnp.zeros((CR, 128), F32)))
            return carry

        lax.fori_loop(0, NB, body, 0)

    def advance(q, carry):
        rows = pl.ds(pl.multiple_of(q * 32, 32), 32)
        total = [8.0 * sums[pl.ds(q * 256 + c, 32, stride=8), :] for c in range(8)]
        position = [st[c, rows, :] for c in range(3)]
        velocity = [st[3 + c, rows, :] for c in range(3)]
        temper, one, two, solid = (st[c, rows, :] for c in range(8, 12))
        vol = total[1]
        temp_one = temper + 0.25 * (total[2] - temper * vol)
        conc_one = one + 0.2 * (total[3] - one * vol)
        conc_two = two + 0.1 * (total[4] - two * vol)
        v_new = [velocity[c] + 0.3 * (total[5 + c] - velocity[c] * vol) for c in range(3)]
        x_new = [position[c] + 0.02 * v_new[c] for c in range(3)]
        liquidus = 1.0 - 0.3 * conc_one - 0.2 * conc_two
        solid_new = jnp.maximum(solid, jnp.clip(2.0 * (liquidus - temp_one), 0.0, 1.0))
        temp_two = temp_one + 0.4 * (solid_new - solid)
        one_new = conc_one * (1.0 - 0.83 * solid) / (1.0 - 0.83 * solid_new)
        two_new = conc_two * (1.0 - 0.6 * solid) / (1.0 - 0.6 * solid_new)
        updated = [*x_new, *v_new, st[6, rows, :], total[0], temp_two, one_new, two_new, solid_new]
        stay = stay_ref[rows, :]
        for c, plane in enumerate(updated):
            kept[c, rows, :] = plane * stay
            upd[pl.ds(q * 512 + c, 32, stride=16), :] = plane
        zero = jnp.zeros((32, 128), F32)
        for c in range(12, 16):
            upd[pl.ds(q * 512 + c, 32, stride=16), :] = zero
        return carry

    lax.fori_loop(0, NB // 32, advance, 0)

    upd[pl.ds(NB * 16, 16), :] = jnp.zeros((16, 128), F32)
    lane = lax.broadcasted_iota(jnp.int32, (16, 128), 1)

    def gather(g, carry):
        acc = jnp.zeros((16, 128), F32)
        for t in range(128):
            m = movers_s[t % 16, g * 8 + t // 16]
            b, ln = lax.shift_right_logical(m, 7), m & 127
            b = jnp.where(t % 16 < counts_s[0, g * 8 + t // 16], b, NB)
            v = upd[pl.ds(pl.multiple_of(b * 16, 16), 16), :]
            acc = jnp.where(lane == t, pltpu.roll(v, (t - ln) & 127, 1), acc)
        for h in range(2):
            message[pl.ds(g * 16 + h, 8, stride=2), :] = swap_groups(acc[8 * h : 8 * h + 8])
        return carry

    lax.fori_loop(0, movers_s.shape[1] // 8, gather, 0)


def local_step(nbr, mask, movers, counts, planes, tables):
    smem, vmem = pl.BlockSpec(memory_space=pltpu.SMEM), pl.BlockSpec(memory_space=pltpu.VMEM)
    doms = movers.shape[1]
    return pl.pallas_call(
        local_kernel,
        out_shape=(
            jax.ShapeDtypeStruct((12, NB, 128), F32),
            pltpu.VMEM((2 * doms, 128), F32),
        ),
        in_specs=[smem] * 4 + [vmem] * 6,
        out_specs=(vmem, vmem),
        scratch_shapes=[
            pltpu.VMEM((NC * 8, 128), F32),
            pltpu.VMEM((NB * 8, 128), F32),
            pltpu.VMEM((NB * 16 + 16, 128), F32),
            *[pltpu.VMEM((128, 512), F32)] * U,
            *[pltpu.VMEM((128, 512), BF16)] * (2 * U),
        ],
        compiler_params=pltpu.CompilerParams(vmem_limit_bytes=VMEM_LIMIT),
    )(nbr, mask, movers, counts, planes, *[pltpu.with_memory_space_constraint(t, pltpu.VMEM) for t in tables])


def migrate_kernel(message, out, first, landed, ssem, rsem):
    grp, me = lax.axis_index("grp"), lax.axis_index("dom")
    y, z, core = me // 16, lax.rem(me // 2, 8), lax.rem(me, 2)
    place = y * 2 + core

    def across(k):
        other = lax.rem(place + k, 8)
        return other // 2, z, lax.rem(other, 2)

    def along(k):
        return y, lax.rem(z + k, 8), core

    def device(at):
        return (grp, at[0] * 16 + at[1] * 2 + at[2])

    barrier = pltpu.get_barrier_semaphore()
    for k in range(1, 8):
        for at in (across(k), along(k)):
            pl.semaphore_signal(barrier, inc=1, device_id=device(at), device_id_type=MESH)
    first[y, core] = message[y, :, core]
    pl.semaphore_wait(barrier, 14)

    def hop_one(k):
        at = across(k)
        return pltpu.make_async_remote_copy(
            src_ref=message.at[at[0], :, at[2]],
            dst_ref=first.at[y, core],
            send_sem=ssem.at[0, k],
            recv_sem=rsem.at[0, k],
            device_id=device(at),
            device_id_type=MESH,
        )

    def hop_two(k):
        at = along(k)
        return pltpu.make_async_remote_copy(
            src_ref=first.at[:, :, at[1]],
            dst_ref=landed.at[:, z],
            send_sem=ssem.at[1, k],
            recv_sem=rsem.at[1, k],
            device_id=device(at),
            device_id_type=MESH,
        )

    one, two = [hop_one(k) for k in range(1, 8)], [hop_two(k) for k in range(1, 8)]
    for copy in one:
        copy.start()
    for copy in one:
        copy.wait_recv()
    for copy in two:
        copy.start()
    landed[:, z] = first[:, :, z]
    for copy in one:
        copy.wait_send()
    for copy in two:
        copy.wait()
    for g in range(8):
        for h in range(2):
            v = landed[g // 2, pl.ds((g % 2) * 4, 4), :, h, :].reshape(8, 128)
            rows = 8 if h == 0 else 4
            out[8 * h : 8 * h + rows, g * 128 : g * 128 + 128] = swap_groups(v)[:rows]


def migrate(message):
    vmem = pl.BlockSpec(memory_space=pltpu.VMEM)
    return pl.pallas_call(
        migrate_kernel,
        out_shape=jax.ShapeDtypeStruct((12, 1024), F32),
        in_specs=[vmem],
        out_specs=vmem,
        scratch_shapes=[
            pltpu.VMEM((4, 2, 8, 2, 128), F32),
            pltpu.VMEM((4, 8, 2, 2, 128), F32),
            pltpu.SemaphoreType.DMA((2, 8)),
            pltpu.SemaphoreType.DMA((2, 8)),
        ],
        compiler_params=pltpu.CompilerParams(
            collective_id=1, has_side_effects=True, vmem_limit_bytes=VMEM_LIMIT
        ),
    )(pltpu.with_memory_space_constraint(message, pltpu.VMEM))


def on_device(state, neighbours, pair_mask, send_lists, send_counts, movers, mover_counts):
    def far(x):
        return pltpu.with_memory_space_constraint(x, pltpu.HBM)

    planes = pltpu.with_memory_space_constraint(state.transpose(1, 0, 2), pltpu.VMEM)
    slots, counts = far(movers[0].T), far(mover_counts)
    tables = exchange(far(send_lists[0]), far(send_counts), planes, slots, counts)
    kept, message = local_step(far(neighbours.T), far(pair_mask.T), slots, counts, planes, tables)
    arrivals = migrate(message.reshape(4, 8, 2, 2, 128))
    return kept.transpose(1, 0, 2), arrivals


def solution(mesh):
    both = ("grp", "dom")
    placed = (P(both, None, None), P(both, None), P(both, None), P(both, None, None), P(both, None), P(both, None, None), P(both, None))
    return jax.shard_map(
        on_device,
        mesh=mesh,
        in_specs=placed,
        out_specs=(P(both, None, None), P(None, both)),
        check_vma=False,
    )
```

```python
import jax
import jax.numpy as jnp
from jax import lax
from jax.experimental import pallas as pl
from jax.experimental.pallas import tpu as pltpu
from jax.sharding import PartitionSpec as P

MESH = pl.DeviceIdType.MESH
F32 = jnp.float32
BF16 = jnp.bfloat16
NB = 256
HB = 64
NC = 512
FR = 48
CR = 32
U = 32
RING = 8
REACH = 2.0
NT = (((1,), (1,)), ((), ()))
TN = (((0,), (0,)), ((), ()))
VMEM_LIMIT = 40 << 20


def carried_planes(st, rows):
    mass = st[6, rows, :]
    volume = mass / st[7, rows, :]
    out = [mass, volume]
    for ch in (8, 9, 10, 3, 4, 5):
        out.append(volume * st[ch, rows, :])
    return out


def pieces(v):
    first = v.astype(BF16).astype(F32)
    rest = v - first
    second = rest.astype(BF16).astype(F32)
    return first, second, rest - second


def exchange_kernel(
    lists, counts, st, movers, mover_counts, halo_x, feat, own_feat, car, stay,
    halo_c, tab_c, tab_x, near_x, tab_p, send_c, pick_x, send_x, ssem, rsem,
):
    grp, dom = lax.axis_index("grp"), lax.axis_index("dom")
    n_grp, n_dom = lax.axis_size("grp"), lax.axis_size("dom")
    has = [dom > 0, dom < n_dom - 1, grp > 0, grp < n_grp - 1]
    peer = [(grp, dom - 1), (grp, dom + 1), (grp - 1, dom), (grp + 1, dom)]
    barrier = pltpu.get_barrier_semaphore()
    for p in range(4):

        @pl.when(has[p])
        def _(p=p):
            pl.semaphore_signal(barrier, inc=1, device_id=peer[p], device_id_type=MESH)

    def build(q, carry):
        rows = pl.ds(pl.multiple_of(q * 32, 32), 32)
        for c, plane in enumerate(carried_planes(st, rows)):
            tab_c[rows, c, :] = plane
        for c in range(3):
            tab_x[rows, c, :] = st[c, rows, :]
        return carry

    lax.fori_loop(0, NB // 32, build, 0)

    def copies(p):
        slot = p ^ 1
        return [
            pltpu.make_async_remote_copy(
                src_ref=send_c.at[pl.ds(p * HB * 8, HB * 8)],
                dst_ref=halo_c.at[pl.ds(slot * HB * 8, HB * 8)],
                send_sem=ssem.at[p, 0],
                recv_sem=rsem.at[slot, 0],
                device_id=peer[p],
                device_id_type=MESH,
            ),
            pltpu.make_async_remote_copy(
                src_ref=send_x.at[:, p],
                dst_ref=halo_x.at[:, pl.ds(slot * HB, HB)],
                send_sem=ssem.at[p, 1],
                recv_sem=rsem.at[slot, 1],
                device_id=peer[p],
                device_id_type=MESH,
            ),
        ]

    met = False
    for p in (3, 2, 1, 0):

        def pick(t, carry, p=p):
            for u in range(8):
                s = t * 8 + u
                live = jnp.where(s < counts[0, p], 1.0, 0.0).astype(F32)
                b = lists[p, s]
                send_c[pl.ds(pl.multiple_of(p * HB * 8 + s * 8, 8), 8), :] = tab_c[b] * live
                pick_x[pl.ds(pl.multiple_of(s * 8, 8), 8), :] = tab_x[b] * live
            return carry

        lax.fori_loop(0, HB // 8, pick, 0)
        for c in range(3):
            send_x[c, p] = pick_x[pl.ds(c, HB, stride=8), :]
        if not met:
            pl.semaphore_wait(barrier, sum(h.astype(jnp.int32) for h in has))
            met = True

        @pl.when(has[p])
        def _(p=p):
            for copy in copies(p):
                copy.start()

    for p in range(4):

        @pl.when(jnp.logical_not(has[p]))
        def _(p=p):
            halo_c[pl.ds(p * HB * 8, HB * 8), :] = jnp.zeros((HB * 8, 128), F32)
            halo_x[:, pl.ds(p * HB, HB), :] = jnp.zeros((3, HB, 128), F32)

    centre = [0.5 * jnp.max(st[c]) + 0.5 * jnp.min(st[c]) for c in range(3)]

    def features(source, own, first, last):
        def body(q, carry):
            rows = pl.ds(pl.multiple_of(q * 32, 32), 32)
            zero, one = jnp.zeros((32, 128), F32), jnp.ones((32, 128), F32)
            norm, xs = None, []
            for c in range(3):
                x = jnp.clip(source[c, rows, :] - centre[c], -REACH - 1.0, REACH + 1.0)
                norm = x * x if norm is None else norm + x * x
                xs.append(x)
            for c, plane in enumerate([*xs, 0.5 - norm, one, zero, zero, zero]):
                near_x[pl.ds(q * 256 + c, 32, stride=8), :] = plane
            if own:
                for c, plane in enumerate([*[2.0 * x for x in xs], one, -norm, zero, zero, zero]):
                    tab_p[pl.ds(q * 256 + c, 32, stride=8), :] = plane
            return carry

        lax.fori_loop(first // 32, last // 32, body, 0)

    def convert(own, first, last):
        def body(q, carry):
            for u in range(8):
                b = q * 8 + u
                at = pl.ds(pl.multiple_of(b * 8, 8), 8)
                n = b if own else b + NB
                x1, x2, x3 = pieces(near_x[at, :])
                feat[n] = jnp.concatenate([x1, x2, x3, x1, x2, x1], 0).astype(BF16)
                c1, c2, c3 = pieces(tab_c[b] if own else halo_c[at, :])
                car[n] = jnp.concatenate([c1, c2, c3, jnp.zeros_like(c1)], 0).astype(BF16)
                if own:
                    p1, p2, p3 = pieces(tab_p[at, :])
                    own_feat[b] = jnp.concatenate([p1, p1, p1, p2, p2, p3], 0).astype(BF16)
            return carry

        lax.fori_loop(first // 8, last // 8, body, 0)

    features(st, True, 0, NB)
    convert(True, 0, NB)
    feat[NC] = jnp.zeros((FR, 128), BF16)
    car[NC] = jnp.zeros((CR, 128), BF16)

    mv = movers[...]
    per = mv.shape[0]
    live = lax.broadcasted_iota(jnp.int32, mv.shape, 0) < mover_counts[...]
    block_of = jnp.where(live, lax.shift_right_logical(mv, 7), -1)
    lane_of = mv & 127
    gone = jnp.zeros((NB, 128), F32)
    for r in range(0, per, 2):
        b = jnp.concatenate([block_of[r : r + 1], block_of[r + 1 : r + 2]], 1)
        ln = jnp.concatenate([lane_of[r : r + 1], lane_of[r + 1 : r + 2]], 1)
        in_block = (lax.broadcasted_iota(jnp.int32, (NB, 128), 0) == b).astype(F32).astype(BF16)
        in_lane = (lax.broadcasted_iota(jnp.int32, (128, 128), 0) == ln).astype(F32).astype(BF16)
        gone = gone + lax.dot_general(in_block, in_lane, NT, preferred_element_type=F32)
    stay[...] = 1.0 - gone

    for p in range(4):

        @pl.when(has[p])
        def _(p=p):
            for copy in copies(p ^ 1):
                copy.wait_recv()

        features(halo_x, False, p * HB, p * HB + HB)
        convert(False, p * HB, p * HB + HB)

    for p in range(4):

        @pl.when(has[p])
        def _(p=p):
            for copy in copies(p):
                copy.wait_send()


def exchange(lists, counts, planes, movers, mover_counts):
    smem, vmem = pl.BlockSpec(memory_space=pltpu.SMEM), pl.BlockSpec(memory_space=pltpu.VMEM)
    return pl.pallas_call(
        exchange_kernel,
        out_shape=(
            pltpu.VMEM((3, 4 * HB, 128), F32),
            pltpu.VMEM((NC + 1, FR, 128), BF16),
            pltpu.VMEM((NB, FR, 128), BF16),
            pltpu.VMEM((NC + 1, CR, 128), BF16),
            pltpu.VMEM((NB, 128), F32),
        ),
        in_specs=[smem, smem, vmem, vmem, vmem],
        out_specs=(vmem,) * 5,
        scratch_shapes=[
            pltpu.VMEM((4 * HB * 8, 128), F32),
            pltpu.VMEM((NB, 8, 128), F32),
            pltpu.VMEM((NB, 8, 128), F32),
            pltpu.VMEM((NB * 8, 128), F32),
            pltpu.VMEM((NB * 8, 128), F32),
            pltpu.VMEM((4 * HB * 8, 128), F32),
            pltpu.VMEM((HB * 8, 128), F32),
            pltpu.VMEM((3, 4, HB, 128), F32),
            pltpu.SemaphoreType.DMA((4, 2)),
            pltpu.SemaphoreType.DMA((4, 2)),
        ],
        compiler_params=pltpu.CompilerParams(
            collective_id=0, has_side_effects=True, vmem_limit_bytes=VMEM_LIMIT
        ),
    )(lists, counts, planes, movers, mover_counts)


def swap_groups(v):
    row = lax.broadcasted_iota(jnp.int32, (8, 128), 0)
    group = lax.broadcasted_iota(jnp.int32, (8, 128), 1) // 16
    apart = (row - group) & 7
    out = v
    for d in range(1, 8):
        moved = pltpu.roll(pltpu.roll(v, d, 0), 128 - 16 * d, 1)
        out = jnp.where(apart == d, moved, out)
    return out


def local_kernel(
    nbr, mask, movers_s, counts_s, st, halo_x, feat, own_feat, car, stay_ref, kept_out, message,
    tab_x, sums, upd, kept, *stages,
):
    dist, parts = stages[:RING], stages[RING:-1]
    wide = None
    for c in range(3):
        half = 0.5 * jnp.max(st[c]) - 0.5 * jnp.min(st[c])
        wide = half if wide is None else jnp.maximum(wide, half)
    close = wide <= REACH

    def slot(k, i):
        return jnp.where(mask[k, i] == 0, NC, nbr[k, i])

    def store_sums(i, r):
        sums[pl.ds(pl.multiple_of(i * 8, 8), 8), :] = r[0:8] + r[8:16] + r[16:24]

    def split(w):
        h = w.astype(BF16)
        return h, (w - h.astype(F32)).astype(BF16)

    def measure(i, u):
        for half in range(2):
            near = jnp.concatenate([feat[slot(2 * half + k, i)] for k in range(2)], 1)
            dist[u][:, half * 256 : half * 256 + 256] = lax.dot_general(
                own_feat[i], near, TN, preferred_element_type=F32
            )

    def weigh(u):
        for half in range(2):
            cols = slice(half * 256, half * 256 + 256)
            s = jnp.maximum(dist[u][:, cols], 0.0)
            h, rest = split(s * s * s)
            parts[u][0:128, cols] = h
            parts[u][128:256, cols] = rest

    def contract(i, u):
        c = jnp.concatenate([car[slot(k, i)] for k in range(4)], 1)
        r = lax.dot_general(c, parts[u][...], NT, preferred_element_type=F32)
        store_sums(i, r[:, 0:128] + r[:, 128:256])

    @pl.when(close)
    def _():
        def body(t, carry):
            for u in range(U):
                i = t * U + u
                contract(jnp.maximum(i - 2, 0), (u - 2) % RING)
                weigh((u - 1) % RING)
                measure(i, u % RING)
            return carry

        lax.fori_loop(0, NB // U, body, 0)
        contract(NB - 2, RING - 2)
        weigh(RING - 1)
        contract(NB - 1, RING - 1)

    @pl.when(jnp.logical_not(close))
    def _():
        def raw(q, carry):
            own = pl.ds(pl.multiple_of(q * 32, 32), 32)
            for c in range(3):
                tab_x[pl.ds(q * 256 + c, 32, stride=8), :] = st[c, own, :]
                tab_x[pl.ds(NB * 8 + q * 256 + c, 32, stride=8), :] = halo_x[c, own, :]
            return carry

        lax.fori_loop(0, NB // 32, raw, 0)

        def body(i, carry):
            columns = jnp.transpose(tab_x[pl.ds(pl.multiple_of(i * 8, 8), 8), :])

            def pair(k, total):
                near = tab_x[pl.ds(pl.multiple_of(nbr[k, i] * 8, 8), 8), :]
                s = jnp.full((128, 128), 0.5, F32)
                for c in range(3):
                    delta = columns[:, c : c + 1] - near[c : c + 1, :]
                    s = s - delta * delta
                s = jnp.maximum(s, 0.0)
                h, rest = split(s * s * s)
                cc = car[slot(k, i)]
                r = lax.dot_general(cc, h, NT, preferred_element_type=F32)
                return total + r + lax.dot_general(cc, rest, NT, preferred_element_type=F32)

            store_sums(i, lax.fori_loop(0, 4, pair, jnp.zeros((CR, 128), F32)))
            return carry

        lax.fori_loop(0, NB, body, 0)

    def advance(q, carry):
        rows = pl.ds(pl.multiple_of(q * 32, 32), 32)
        total = [8.0 * sums[pl.ds(q * 256 + c, 32, stride=8), :] for c in range(8)]
        position = [st[c, rows, :] for c in range(3)]
        velocity = [st[3 + c, rows, :] for c in range(3)]
        temper, one, two, solid = (st[c, rows, :] for c in range(8, 12))
        vol = total[1]
        temp_one = temper + 0.25 * (total[2] - temper * vol)
        conc_one = one + 0.2 * (total[3] - one * vol)
        conc_two = two + 0.1 * (total[4] - two * vol)
        v_new = [velocity[c] + 0.3 * (total[5 + c] - velocity[c] * vol) for c in range(3)]
        x_new = [position[c] + 0.02 * v_new[c] for c in range(3)]
        liquidus = 1.0 - 0.3 * conc_one - 0.2 * conc_two
        solid_new = jnp.maximum(solid, jnp.clip(2.0 * (liquidus - temp_one), 0.0, 1.0))
        temp_two = temp_one + 0.4 * (solid_new - solid)
        one_new = conc_one * (1.0 - 0.83 * solid) / (1.0 - 0.83 * solid_new)
        two_new = conc_two * (1.0 - 0.6 * solid) / (1.0 - 0.6 * solid_new)
        updated = [*x_new, *v_new, st[6, rows, :], total[0], temp_two, one_new, two_new, solid_new]
        stay = stay_ref[rows, :]
        for c, plane in enumerate(updated):
            kept[c, rows, :] = plane * stay
            upd[pl.ds(q * 512 + c, 32, stride=16), :] = plane
        zero = jnp.zeros((32, 128), F32)
        for c in range(12, 16):
            upd[pl.ds(q * 512 + c, 32, stride=16), :] = zero
        return carry

    lax.fori_loop(0, NB // 32, advance, 0)

    out_copy = pltpu.make_async_copy(kept, kept_out, stages[-1])
    out_copy.start()
    lane = lax.broadcasted_iota(jnp.int32, (16, 128), 1)

    def gather(g, carry):
        count = jnp.zeros((16, 128), jnp.int32)
        for q in range(8):
            count = jnp.where(lax.shift_right_logical(lane, 4) == q, counts_s[0, g * 8 + q], count)
        acc = jnp.zeros((16, 128), F32)
        for t in range(128):
            m = movers_s[t % 16, g * 8 + t // 16]
            at = pl.multiple_of(lax.shift_right_logical(m, 7) * 16, 16)
            acc = jnp.where(lane == t, pltpu.roll(upd[pl.ds(at, 16), :], (t - m) & 127, 1), acc)
        acc = jnp.where((lane & 15) < count, acc, 0.0)
        for h in range(2):
            message[pl.ds(g * 16 + h, 8, stride=2), :] = swap_groups(acc[8 * h : 8 * h + 8])
        return carry

    lax.fori_loop(0, movers_s.shape[1] // 8, gather, 0)
    out_copy.wait()


def local_step(nbr, mask, movers, counts, planes, tables):
    smem, vmem = pl.BlockSpec(memory_space=pltpu.SMEM), pl.BlockSpec(memory_space=pltpu.VMEM)
    doms = movers.shape[1]
    return pl.pallas_call(
        local_kernel,
        out_shape=(
            pltpu.HBM((12, NB, 128), F32),
            pltpu.VMEM((2 * doms, 128), F32),
        ),
        in_specs=[smem] * 4 + [vmem] * 6,
        out_specs=(pl.BlockSpec(memory_space=pl.ANY), vmem),
        scratch_shapes=[
            pltpu.VMEM((NC * 8, 128), F32),
            pltpu.VMEM((NB * 8, 128), F32),
            pltpu.VMEM((NB * 16, 128), F32),
            pltpu.VMEM((12, NB, 128), F32),
            *[pltpu.VMEM((128, 512), F32)] * RING,
            *[pltpu.VMEM((256, 512), BF16)] * RING,
            pltpu.SemaphoreType.DMA,
        ],
        compiler_params=pltpu.CompilerParams(vmem_limit_bytes=VMEM_LIMIT),
    )(nbr, mask, movers, counts, planes, *[pltpu.with_memory_space_constraint(t, pltpu.VMEM) for t in tables])


def migrate_kernel(message, out, first, landed, ssem, rsem):
    grp, me = lax.axis_index("grp"), lax.axis_index("dom")
    y, z, core = me // 16, lax.rem(me // 2, 8), lax.rem(me, 2)
    place = y * 2 + core

    def across(k):
        other = lax.rem(place + k, 8)
        return other // 2, z, lax.rem(other, 2)

    def along(k):
        return y, lax.rem(z + k, 8), core

    def device(at):
        return (grp, at[0] * 16 + at[1] * 2 + at[2])

    barrier = pltpu.get_barrier_semaphore()
    for k in range(1, 8):
        for at in (across(k), along(k)):
            pl.semaphore_signal(barrier, inc=1, device_id=device(at), device_id_type=MESH)
    first[y, core] = message[y, :, core]
    pl.semaphore_wait(barrier, 14)

    def hop_one(k):
        at = across(k)
        return pltpu.make_async_remote_copy(
            src_ref=message.at[at[0], :, at[2]],
            dst_ref=first.at[y, core],
            send_sem=ssem.at[0, k],
            recv_sem=rsem.at[0, k],
            device_id=device(at),
            device_id_type=MESH,
        )

    def hop_two(k):
        at = along(k)
        return pltpu.make_async_remote_copy(
            src_ref=first.at[:, :, at[1]],
            dst_ref=landed.at[:, z],
            send_sem=ssem.at[1, k],
            recv_sem=rsem.at[1, k],
            device_id=device(at),
            device_id_type=MESH,
        )

    one, two = [hop_one(k) for k in range(1, 8)], [hop_two(k) for k in range(1, 8)]
    for copy in one:
        copy.start()
    for copy in one:
        copy.wait_recv()
    for copy in two:
        copy.start()
    landed[:, z] = first[:, :, z]
    for copy in one:
        copy.wait_send()
    for copy in two:
        copy.wait()
    for g in range(8):
        for h in range(2):
            v = landed[g // 2, pl.ds((g % 2) * 4, 4), :, h, :].reshape(8, 128)
            rows = 8 if h == 0 else 4
            out[8 * h : 8 * h + rows, g * 128 : g * 128 + 128] = swap_groups(v)[:rows]


def migrate(message):
    vmem = pl.BlockSpec(memory_space=pltpu.VMEM)
    return pl.pallas_call(
        migrate_kernel,
        out_shape=jax.ShapeDtypeStruct((12, 1024), F32),
        in_specs=[vmem],
        out_specs=vmem,
        scratch_shapes=[
            pltpu.VMEM((4, 2, 8, 2, 128), F32),
            pltpu.VMEM((4, 8, 2, 2, 128), F32),
            pltpu.SemaphoreType.DMA((2, 8)),
            pltpu.SemaphoreType.DMA((2, 8)),
        ],
        compiler_params=pltpu.CompilerParams(
            collective_id=1, has_side_effects=True, vmem_limit_bytes=VMEM_LIMIT
        ),
    )(pltpu.with_memory_space_constraint(message, pltpu.VMEM))


def on_device(state, neighbours, pair_mask, send_lists, send_counts, movers, mover_counts):
    def far(x):
        return pltpu.with_memory_space_constraint(x, pltpu.HBM)

    planes = pltpu.with_memory_space_constraint(state.transpose(1, 0, 2), pltpu.VMEM)
    slots, counts = far(movers[0].T), far(mover_counts)
    tables = exchange(far(send_lists[0]), far(send_counts), planes, slots, counts)
    kept, message = local_step(far(neighbours.T), far(pair_mask.T), slots, counts, planes, tables)
    arrivals = migrate(message.reshape(4, 8, 2, 2, 128))
    return kept.transpose(1, 0, 2), arrivals


def solution(mesh):
    both = ("grp", "dom")
    placed = (P(both, None, None), P(both, None), P(both, None), P(both, None, None), P(both, None), P(both, None, None), P(both, None))
    return jax.shard_map(
        on_device,
        mesh=mesh,
        in_specs=placed,
        out_specs=(P(both, None, None), P(None, both)),
        check_vma=False,
    )
```

```python
import jax
import jax.numpy as jnp
from jax import lax
from jax.experimental import pallas as pl
from jax.experimental.pallas import tpu as pltpu
from jax.sharding import PartitionSpec as P

MESH = pl.DeviceIdType.MESH
F32 = jnp.float32
BF16 = jnp.bfloat16
NB = 256
HB = 64
NC = 512
FR = 48
CR = 32
U = 32
UA = 8
RB = 4
REACH = 2.0
NT = (((1,), (1,)), ((), ()))
TN = (((0,), (0,)), ((), ()))
VMEM_LIMIT = 40 << 20


def carried_planes(st, rows):
    mass = st[6, rows, :]
    volume = mass / st[7, rows, :]
    out = [mass, volume]
    for ch in (8, 9, 10, 3, 4, 5):
        out.append(volume * st[ch, rows, :])
    return out


def split(w):
    h = w.astype(BF16)
    return h, (w - h.astype(F32)).astype(BF16)


def weights(dist, lane, row, parts, out_row):
    s = jnp.maximum(dist[row : row + 128, lane : lane + 128], 0.0)
    h, rest = split(s * s * s)
    parts[out_row : out_row + 128, 0:128] = h
    parts[out_row : out_row + 128, 128:256] = rest


def beside(one, two):
    return jnp.concatenate(
        [
            jnp.concatenate([one, jnp.zeros_like(two)], 1),
            jnp.concatenate([jnp.zeros_like(one), two], 1),
        ],
        0,
    )


def fold(r):
    r = r[:, 0:128] + r[:, 128:256]
    return r[0:8] + r[8:16] + r[16:24]


def pieces(v):
    first = v.astype(BF16).astype(F32)
    rest = v - first
    second = rest.astype(BF16).astype(F32)
    return first, second, rest - second


def order_slots(nbr, mask):
    a, b, c, d = (jnp.where(mask[k : k + 1, :] == 0, NC, nbr[k : k + 1, :]) for k in range(4))
    which = jnp.full_like(a, 4)
    for k, slots in ((3, d), (2, c), (1, b), (0, a)):
        which = jnp.where((slots < NB) | (slots == NC), k, which)
    first = jnp.where(which == 0, a, jnp.where(which == 1, b, jnp.where(which == 2, c, d)))
    rows = [
        jnp.where(which == 4, NC, first),
        jnp.where(which == 0, b, a),
        jnp.where(which <= 1, c, b),
        jnp.where(which <= 2, d, c),
        jnp.where(which == 4, d, NC),
    ]
    return jnp.concatenate(rows + [jnp.full_like(a, NC)] * 3, 0)


def exchange_kernel(
    lists, counts, st, movers, mover_counts, nbr, mask, halo_x, feat, own_feat, car, stay, near_sums, order_out,
    halo_c, tab_c, tab_x, near_x, tab_p, send_c, pick_x, send_x, ssem, rsem, order, order_sem, *stages,
):
    grp, dom = lax.axis_index("grp"), lax.axis_index("dom")
    n_grp, n_dom = lax.axis_size("grp"), lax.axis_size("dom")
    has = [dom > 0, dom < n_dom - 1, grp > 0, grp < n_grp - 1]
    peer = [(grp, dom - 1), (grp, dom + 1), (grp - 1, dom), (grp + 1, dom)]
    barrier = pltpu.get_barrier_semaphore()
    for p in range(4):

        @pl.when(has[p])
        def _(p=p):
            pl.semaphore_signal(barrier, inc=1, device_id=peer[p], device_id_type=MESH)

    def build(q, carry):
        rows = pl.ds(pl.multiple_of(q * 32, 32), 32)
        for c, plane in enumerate(carried_planes(st, rows)):
            tab_c[rows, c, :] = plane
        for c in range(3):
            tab_x[rows, c, :] = st[c, rows, :]
        return carry

    lax.fori_loop(0, NB // 32, build, 0)

    def copies(p):
        slot = p ^ 1
        return [
            pltpu.make_async_remote_copy(
                src_ref=send_c.at[pl.ds(p * HB * 8, HB * 8)],
                dst_ref=halo_c.at[pl.ds(slot * HB * 8, HB * 8)],
                send_sem=ssem.at[p, 0],
                recv_sem=rsem.at[slot, 0],
                device_id=peer[p],
                device_id_type=MESH,
            ),
            pltpu.make_async_remote_copy(
                src_ref=send_x.at[:, p],
                dst_ref=halo_x.at[:, pl.ds(slot * HB, HB)],
                send_sem=ssem.at[p, 1],
                recv_sem=rsem.at[slot, 1],
                device_id=peer[p],
                device_id_type=MESH,
            ),
        ]

    met = False
    for p in (3, 2, 1, 0):

        def pick(t, carry, p=p):
            for u in range(8):
                s = t * 8 + u
                live = jnp.where(s < counts[0, p], 1.0, 0.0).astype(F32)
                b = lists[p, s]
                send_c[pl.ds(pl.multiple_of(p * HB * 8 + s * 8, 8), 8), :] = tab_c[b] * live
                pick_x[pl.ds(pl.multiple_of(s * 8, 8), 8), :] = tab_x[b] * live
            return carry

        lax.fori_loop(0, HB // 8, pick, 0)
        for c in range(3):
            send_x[c, p] = pick_x[pl.ds(c, HB, stride=8), :]
        if not met:
            pl.semaphore_wait(barrier, sum(h.astype(jnp.int32) for h in has))
            met = True

        @pl.when(has[p])
        def _(p=p):
            for copy in copies(p):
                copy.start()

    for p in range(4):

        @pl.when(jnp.logical_not(has[p]))
        def _(p=p):
            halo_c[pl.ds(p * HB * 8, HB * 8), :] = jnp.zeros((HB * 8, 128), F32)
            halo_x[:, pl.ds(p * HB, HB), :] = jnp.zeros((3, HB, 128), F32)

    centre = [0.5 * jnp.max(st[c]) + 0.5 * jnp.min(st[c]) for c in range(3)]

    def features(source, own, first, last):
        def body(q, carry):
            rows = pl.ds(pl.multiple_of(q * 32, 32), 32)
            zero, one = jnp.zeros((32, 128), F32), jnp.ones((32, 128), F32)
            norm, xs = None, []
            for c in range(3):
                x = jnp.clip(source[c, rows, :] - centre[c], -REACH - 1.0, REACH + 1.0)
                norm = x * x if norm is None else norm + x * x
                xs.append(x)
            for c, plane in enumerate([*xs, 0.5 - norm, one, zero, zero, zero]):
                near_x[pl.ds(q * 256 + c, 32, stride=8), :] = plane
            if own:
                for c, plane in enumerate([*[2.0 * x for x in xs], one, -norm, zero, zero, zero]):
                    tab_p[pl.ds(q * 256 + c, 32, stride=8), :] = plane
            return carry

        lax.fori_loop(first // 32, last // 32, body, 0)

    def convert(own, first, last):
        def body(q, carry):
            for u in range(8):
                b = q * 8 + u
                at = pl.ds(pl.multiple_of(b * 8, 8), 8)
                n = b if own else b + NB
                x1, x2, x3 = pieces(near_x[at, :])
                feat[n] = jnp.concatenate([x1, x2, x3, x1, x2, x1], 0).astype(BF16)
                c1, c2, c3 = pieces(tab_c[b] if own else halo_c[at, :])
                car[n] = jnp.concatenate([c1, c2, c3, jnp.zeros_like(c1)], 0).astype(BF16)
                if own:
                    p1, p2, p3 = pieces(tab_p[at, :])
                    own_feat[b] = jnp.concatenate([p1, p1, p1, p2, p2, p3], 0).astype(BF16)
            return carry

        lax.fori_loop(first // 8, last // 8, body, 0)

    order_out[...] = order_slots(nbr, mask)
    order_copy = pltpu.make_async_copy(order_out, order, order_sem)
    order_copy.start()
    features(st, True, 0, NB)
    convert(True, 0, NB)
    feat[NC] = jnp.zeros((FR, 128), BF16)
    car[NC] = jnp.zeros((CR, 128), BF16)

    mv = movers[...]
    per = mv.shape[0]
    live = lax.broadcasted_iota(jnp.int32, mv.shape, 0) < mover_counts[...]
    block_of = jnp.where(live, lax.shift_right_logical(mv, 7), -1)
    lane_of = mv & 127
    gone = jnp.zeros((NB, 128), F32)
    for r in range(0, per, 2):
        b = jnp.concatenate([block_of[r : r + 1], block_of[r + 1 : r + 2]], 1)
        ln = jnp.concatenate([lane_of[r : r + 1], lane_of[r + 1 : r + 2]], 1)
        in_block = (lax.broadcasted_iota(jnp.int32, (NB, 128), 0) == b).astype(F32).astype(BF16)
        in_lane = (lax.broadcasted_iota(jnp.int32, (128, 128), 0) == ln).astype(F32).astype(BF16)
        gone = gone + lax.dot_general(in_block, in_lane, NT, preferred_element_type=F32)
    stay[...] = 1.0 - gone

    dist, parts = stages[:RB], stages[RB:]

    def measure(p, u):
        one, two = 2 * p, 2 * p + 1
        near = jnp.concatenate([feat[order[0, one]], feat[order[0, two]]], 0)
        dist[u][...] = lax.dot_general(
            near, beside(own_feat[one], own_feat[two]), TN, preferred_element_type=F32
        )

    def weigh(u):
        for n in range(2):
            weights(dist[u], n * 128, 0, parts[u], n * 128)

    def contract(p, u):
        c = beside(car[order[0, 2 * p]], car[order[0, 2 * p + 1]])
        r = jnp.dot(c, parts[u][...], preferred_element_type=F32)
        at = pl.multiple_of(p * 16, 16)
        near_sums[pl.ds(at, 8), :] = fold(r[0:CR])
        near_sums[pl.ds(at + 8, 8), :] = fold(r[CR:])

    order_copy.wait()
    measure(0, 0)
    weigh(0)
    measure(1, 1)

    def steps(t, last):
        for u in range(UA):
            p = t * UA + u
            contract(p, u % RB)
            if not last or u < UA - 1:
                weigh((u + 1) % RB)
            if not last or u < UA - 2:
                measure(p + 2, (u + 2) % RB)

    def body(t, carry):
        steps(t, False)
        return carry

    lax.fori_loop(0, NB // 2 // UA - 1, body, 0)
    steps(NB // 2 // UA - 1, True)

    for p in range(4):

        @pl.when(has[p])
        def _(p=p):
            for copy in copies(p ^ 1):
                copy.wait_recv()

        features(halo_x, False, p * HB, p * HB + HB)
        convert(False, p * HB, p * HB + HB)

    for p in range(4):

        @pl.when(has[p])
        def _(p=p):
            for copy in copies(p):
                copy.wait_send()


def exchange(lists, counts, planes, movers, mover_counts, nbr, mask):
    smem, vmem = pl.BlockSpec(memory_space=pltpu.SMEM), pl.BlockSpec(memory_space=pltpu.VMEM)
    return pl.pallas_call(
        exchange_kernel,
        out_shape=(
            pltpu.VMEM((3, 4 * HB, 128), F32),
            pltpu.VMEM((NC + 1, FR, 128), BF16),
            pltpu.VMEM((NB, FR, 128), BF16),
            pltpu.VMEM((NC + 1, CR, 128), BF16),
            pltpu.VMEM((NB, 128), F32),
            pltpu.VMEM((NB * 8, 128), F32),
            pltpu.VMEM((8, NB), jnp.int32),
        ),
        in_specs=[smem, smem] + [vmem] * 5,
        out_specs=(vmem,) * 7,
        scratch_shapes=[
            pltpu.VMEM((4 * HB * 8, 128), F32),
            pltpu.VMEM((NB, 8, 128), F32),
            pltpu.VMEM((NB, 8, 128), F32),
            pltpu.VMEM((NB * 8, 128), F32),
            pltpu.VMEM((NB * 8, 128), F32),
            pltpu.VMEM((4 * HB * 8, 128), F32),
            pltpu.VMEM((HB * 8, 128), F32),
            pltpu.VMEM((3, 4, HB, 128), F32),
            pltpu.SemaphoreType.DMA((4, 2)),
            pltpu.SemaphoreType.DMA((4, 2)),
            pltpu.SMEM((8, NB), jnp.int32),
            pltpu.SemaphoreType.DMA,
            *[pltpu.VMEM((128, 256), F32)] * RB,
            *[pltpu.VMEM((256, 256), BF16)] * RB,
        ],
        compiler_params=pltpu.CompilerParams(
            collective_id=0, has_side_effects=True, vmem_limit_bytes=VMEM_LIMIT
        ),
    )(lists, counts, planes, movers, mover_counts, nbr, mask)


def swap_groups(v):
    row = lax.broadcasted_iota(jnp.int32, (8, 128), 0)
    group = lax.broadcasted_iota(jnp.int32, (8, 128), 1) // 16
    apart = (row - group) & 7
    out = v
    for d in range(1, 8):
        moved = pltpu.roll(pltpu.roll(v, d, 0), 128 - 16 * d, 1)
        out = jnp.where(apart == d, moved, out)
    return out


def local_kernel(
    order, nbr, mask, movers_s, counts_s, st, halo_x, feat, own_feat, car, stay_ref, near_sums, kept_out, message,
    tab_x, sums, upd, kept, late, *stages,
):
    dist, parts = stages[:RB], stages[RB:-1]
    wide = None
    for c in range(3):
        half = 0.5 * jnp.max(st[c]) - 0.5 * jnp.min(st[c])
        wide = half if wide is None else jnp.maximum(wide, half)
    close = wide <= REACH

    def measure(p, u):
        one, two = 2 * p, 2 * p + 1
        mine = beside(own_feat[one], own_feat[two])
        for k in range(3):
            near = jnp.concatenate([feat[order[k + 1, one]], feat[order[k + 1, two]]], 0)
            dist[u][k * 128 : k * 128 + 128, :] = lax.dot_general(
                near, mine, TN, preferred_element_type=F32
            )

    def weigh(u):
        for n in range(2):
            for k in range(3):
                weights(dist[u], n * 128, k * 128, parts[u], (n * 3 + k) * 128)

    def contract(p, u):
        c = beside(*[
            jnp.concatenate([car[order[k, i]] for k in (1, 2, 3)], 1) for i in (2 * p, 2 * p + 1)
        ])
        r = jnp.dot(c, parts[u][...], preferred_element_type=F32)
        at = pl.multiple_of(p * 16, 16)
        sums[pl.ds(at, 8), :] = fold(r[0:CR])
        sums[pl.ds(at + 8, 8), :] = fold(r[CR:])

    @pl.when(close)
    def _():
        def body(t, n_late):
            for u in range(U):
                p = t * U + u
                for i in (2 * p, 2 * p + 1):
                    late[n_late] = i
                    n_late = n_late + jnp.where(order[4, i] == NC, 0, 1)
                contract(jnp.maximum(p - 2, 0), (u - 2) % RB)
                weigh((u - 1) % RB)
                measure(p, u % RB)
            return n_late

        n_late = lax.fori_loop(0, NB // 2 // U, body, 0)
        contract(NB // 2 - 2, RB - 2)
        weigh(RB - 1)
        contract(NB // 2 - 1, RB - 1)

        def rest(t, carry):
            blocks, slots = [], []
            for u in range(2 * RB):
                on = t * 2 * RB + u < n_late
                blocks.append(jnp.where(on, late[t * 2 * RB + u], 0))
                slots.append(jnp.where(on, order[4, blocks[u]], NC))
                lanes = slice((u % 2) * 128, (u % 2) * 128 + 128)
                dist[u // 2][0:128, lanes] = lax.dot_general(
                    feat[slots[u]], own_feat[blocks[u]], TN, preferred_element_type=F32
                )
            for u in range(2 * RB):
                weights(dist[u // 2], (u % 2) * 128, 0, parts[u // 2], (u % 2) * 128)
            for u in range(2 * RB):
                rows = slice((u % 2) * 128, (u % 2) * 128 + 128)
                r = jnp.dot(car[slots[u]], parts[u // 2][rows, :], preferred_element_type=F32)
                at = pl.ds(pl.multiple_of(blocks[u] * 8, 8), 8)
                sums[at, :] = sums[at, :] + fold(r)
            return carry

        lax.fori_loop(0, (n_late + 2 * RB - 1) // (2 * RB), rest, 0)

        def add(q, carry):
            at = pl.ds(pl.multiple_of(q * 256, 256), 256)
            sums[at, :] = sums[at, :] + near_sums[at, :]
            return carry

        lax.fori_loop(0, NB // 32, add, 0)

    @pl.when(jnp.logical_not(close))
    def _():
        def raw(q, carry):
            own = pl.ds(pl.multiple_of(q * 32, 32), 32)
            for c in range(3):
                tab_x[pl.ds(q * 256 + c, 32, stride=8), :] = st[c, own, :]
                tab_x[pl.ds(NB * 8 + q * 256 + c, 32, stride=8), :] = halo_x[c, own, :]
            return carry

        lax.fori_loop(0, NB // 32, raw, 0)

        def body(i, carry):
            columns = jnp.transpose(tab_x[pl.ds(pl.multiple_of(i * 8, 8), 8), :])

            def pair(k, total):
                near = tab_x[pl.ds(pl.multiple_of(nbr[k, i] * 8, 8), 8), :]
                s = jnp.full((128, 128), 0.5, F32)
                for c in range(3):
                    delta = columns[:, c : c + 1] - near[c : c + 1, :]
                    s = s - delta * delta
                s = jnp.maximum(s, 0.0)
                h, rest = split(s * s * s)
                cc = car[jnp.where(mask[k, i] == 0, NC, nbr[k, i])]
                return total + lax.dot_general(cc, jnp.concatenate([h, rest], 0), NT, preferred_element_type=F32)

            total = lax.fori_loop(0, 4, pair, jnp.zeros((CR, 256), F32))
            sums[pl.ds(pl.multiple_of(i * 8, 8), 8), :] = fold(total)
            return carry

        lax.fori_loop(0, NB, body, 0)

    def advance(q, carry):
        rows = pl.ds(pl.multiple_of(q * 32, 32), 32)
        total = [8.0 * sums[pl.ds(q * 256 + c, 32, stride=8), :] for c in range(8)]
        position = [st[c, rows, :] for c in range(3)]
        velocity = [st[3 + c, rows, :] for c in range(3)]
        temper, one, two, solid = (st[c, rows, :] for c in range(8, 12))
        vol = total[1]
        temp_one = temper + 0.25 * (total[2] - temper * vol)
        conc_one = one + 0.2 * (total[3] - one * vol)
        conc_two = two + 0.1 * (total[4] - two * vol)
        v_new = [velocity[c] + 0.3 * (total[5 + c] - velocity[c] * vol) for c in range(3)]
        x_new = [position[c] + 0.02 * v_new[c] for c in range(3)]
        liquidus = 1.0 - 0.3 * conc_one - 0.2 * conc_two
        solid_new = jnp.maximum(solid, jnp.clip(2.0 * (liquidus - temp_one), 0.0, 1.0))
        temp_two = temp_one + 0.4 * (solid_new - solid)
        one_new = conc_one * (1.0 - 0.83 * solid) / (1.0 - 0.83 * solid_new)
        two_new = conc_two * (1.0 - 0.6 * solid) / (1.0 - 0.6 * solid_new)
        updated = [*x_new, *v_new, st[6, rows, :], total[0], temp_two, one_new, two_new, solid_new]
        stay = stay_ref[rows, :]
        for c, plane in enumerate(updated):
            kept[c, rows, :] = plane * stay
            upd[pl.ds(q * 512 + c, 32, stride=16), :] = plane
        zero = jnp.zeros((32, 128), F32)
        for c in range(12, 16):
            upd[pl.ds(q * 512 + c, 32, stride=16), :] = zero
        return carry

    lax.fori_loop(0, NB // 32, advance, 0)

    out_copy = pltpu.make_async_copy(kept, kept_out, stages[-1])
    out_copy.start()
    lane = lax.broadcasted_iota(jnp.int32, (16, 128), 1)

    def gather(g, carry):
        count = jnp.zeros((16, 128), jnp.int32)
        for q in range(8):
            count = jnp.where(lax.shift_right_logical(lane, 4) == q, counts_s[0, g * 8 + q], count)
        acc = jnp.zeros((16, 128), F32)
        for t in range(128):
            m = movers_s[t % 16, g * 8 + t // 16]
            at = pl.multiple_of(lax.shift_right_logical(m, 7) * 16, 16)
            acc = jnp.where(lane == t, pltpu.roll(upd[pl.ds(at, 16), :], (t - m) & 127, 1), acc)
        acc = jnp.where((lane & 15) < count, acc, 0.0)
        for h in range(2):
            message[pl.ds(g * 16 + h, 8, stride=2), :] = swap_groups(acc[8 * h : 8 * h + 8])
        return carry

    lax.fori_loop(0, movers_s.shape[1] // 8, gather, 0)
    out_copy.wait()


def local_step(order, nbr, mask, movers, counts, planes, tables):
    smem, vmem = pl.BlockSpec(memory_space=pltpu.SMEM), pl.BlockSpec(memory_space=pltpu.VMEM)
    doms = movers.shape[1]
    return pl.pallas_call(
        local_kernel,
        out_shape=(
            pltpu.HBM((12, NB, 128), F32),
            pltpu.VMEM((2 * doms, 128), F32),
        ),
        in_specs=[smem] * 5 + [vmem] * 7,
        out_specs=(pl.BlockSpec(memory_space=pl.ANY), vmem),
        scratch_shapes=[
            pltpu.VMEM((NC * 8, 128), F32),
            pltpu.VMEM((NB * 8, 128), F32),
            pltpu.VMEM((NB * 16, 128), F32),
            pltpu.VMEM((12, NB, 128), F32),
            pltpu.SMEM((NB + 4 * RB,), jnp.int32),
            *[pltpu.VMEM((384, 256), F32)] * RB,
            *[pltpu.VMEM((768, 256), BF16)] * RB,
            pltpu.SemaphoreType.DMA,
        ],
        compiler_params=pltpu.CompilerParams(vmem_limit_bytes=VMEM_LIMIT),
    )(pltpu.with_memory_space_constraint(order, pltpu.VMEM), nbr, mask, movers, counts, planes, *[pltpu.with_memory_space_constraint(t, pltpu.VMEM) for t in tables])


def migrate_kernel(message, out, first, landed, ssem, rsem):
    grp, me = lax.axis_index("grp"), lax.axis_index("dom")
    y, z, core = me // 16, lax.rem(me // 2, 8), lax.rem(me, 2)
    place = y * 2 + core

    def across(k):
        other = lax.rem(place + k, 8)
        return other // 2, z, lax.rem(other, 2)

    def along(k):
        return y, lax.rem(z + k, 8), core

    def device(at):
        return (grp, at[0] * 16 + at[1] * 2 + at[2])

    barrier = pltpu.get_barrier_semaphore()
    for k in range(1, 8):
        for at in (across(k), along(k)):
            pl.semaphore_signal(barrier, inc=1, device_id=device(at), device_id_type=MESH)
    first[y, core] = message[y, :, core]
    pl.semaphore_wait(barrier, 14)

    def hop_one(k):
        at = across(k)
        return pltpu.make_async_remote_copy(
            src_ref=message.at[at[0], :, at[2]],
            dst_ref=first.at[y, core],
            send_sem=ssem.at[0, k],
            recv_sem=rsem.at[0, k],
            device_id=device(at),
            device_id_type=MESH,
        )

    def hop_two(k):
        at = along(k)
        return pltpu.make_async_remote_copy(
            src_ref=first.at[:, :, at[1]],
            dst_ref=landed.at[:, z],
            send_sem=ssem.at[1, k],
            recv_sem=rsem.at[1, k],
            device_id=device(at),
            device_id_type=MESH,
        )

    one, two = [hop_one(k) for k in range(1, 8)], [hop_two(k) for k in range(1, 8)]
    for copy in one:
        copy.start()
    for copy in one:
        copy.wait_recv()
    for copy in two:
        copy.start()
    landed[:, z] = first[:, :, z]
    for copy in one:
        copy.wait_send()
    for copy in two:
        copy.wait()
    for g in range(8):
        for h in range(2):
            v = landed[g // 2, pl.ds((g % 2) * 4, 4), :, h, :].reshape(8, 128)
            rows = 8 if h == 0 else 4
            out[8 * h : 8 * h + rows, g * 128 : g * 128 + 128] = swap_groups(v)[:rows]


def migrate(message):
    vmem = pl.BlockSpec(memory_space=pltpu.VMEM)
    return pl.pallas_call(
        migrate_kernel,
        out_shape=jax.ShapeDtypeStruct((12, 1024), F32),
        in_specs=[vmem],
        out_specs=vmem,
        scratch_shapes=[
            pltpu.VMEM((4, 2, 8, 2, 128), F32),
            pltpu.VMEM((4, 8, 2, 2, 128), F32),
            pltpu.SemaphoreType.DMA((2, 8)),
            pltpu.SemaphoreType.DMA((2, 8)),
        ],
        compiler_params=pltpu.CompilerParams(
            collective_id=1, has_side_effects=True, vmem_limit_bytes=VMEM_LIMIT
        ),
    )(pltpu.with_memory_space_constraint(message, pltpu.VMEM))


def on_device(state, neighbours, pair_mask, send_lists, send_counts, movers, mover_counts):
    def far(x):
        return pltpu.with_memory_space_constraint(x, pltpu.HBM)

    planes = pltpu.with_memory_space_constraint(state.transpose(1, 0, 2), pltpu.VMEM)
    slots, counts = far(movers[0].T), far(mover_counts)
    nbr, mask = far(neighbours.T), far(pair_mask.T)
    *tables, order = exchange(far(send_lists[0]), far(send_counts), planes, slots, counts, nbr, mask)
    kept, message = local_step(order, nbr, mask, slots, counts, planes, tables)
    arrivals = migrate(message.reshape(4, 8, 2, 2, 128))
    return kept.transpose(1, 0, 2), arrivals


def solution(mesh):
    both = ("grp", "dom")
    placed = (P(both, None, None), P(both, None), P(both, None), P(both, None, None), P(both, None), P(both, None, None), P(both, None))
    return jax.shard_map(
        on_device,
        mesh=mesh,
        in_specs=placed,
        out_specs=(P(both, None, None), P(None, both)),
        check_vma=False,
    )
```

```python
import jax
import jax.numpy as jnp
from jax import lax
from jax.experimental import pallas as pl
from jax.experimental.pallas import tpu as pltpu
from jax.sharding import PartitionSpec as P

MESH = pl.DeviceIdType.MESH
F32 = jnp.float32
BF16 = jnp.bfloat16
NB = 256
HB = 64
NC = 512
FR = 48
CR = 32
U = 32
RB = 4
LOADS = 4
REACH = 2.0
NT = (((1,), (1,)), ((), ()))
TN = (((0,), (0,)), ((), ()))
VMEM_LIMIT = 40 << 20


def carried_planes(st, rows):
    mass = st[6, rows, :]
    volume = mass / st[7, rows, :]
    out = [mass, volume]
    for ch in (8, 9, 10, 3, 4, 5):
        out.append(volume * st[ch, rows, :])
    return out


def split(w):
    h = w.astype(BF16)
    return h, (w - h.astype(F32)).astype(BF16)


def weights(dist, lane, row, parts, out_row):
    s = jnp.maximum(dist[row : row + 128, lane : lane + 128], 0.0)
    h, rest = split(s * s * s)
    parts[out_row : out_row + 128, 0:128] = h
    parts[out_row : out_row + 128, 128:256] = rest


def beside(one, two):
    return jnp.concatenate(
        [
            jnp.concatenate([one, jnp.zeros_like(two)], 1),
            jnp.concatenate([jnp.zeros_like(one), two], 1),
        ],
        0,
    )


def fold(r):
    r = r[:, 0:128] + r[:, 128:256]
    return r[0:8] + r[8:16] + r[16:24]


def pieces(v):
    first = v.astype(BF16).astype(F32)
    rest = v - first
    second = rest.astype(BF16).astype(F32)
    return first, second, rest - second


def exchange_kernel(
    lists, counts, state, movers, mover_counts, halo_x, feat, own_feat, car, stay, st,
    halo_c, tab_c, tab_x, near_x, tab_p, send_c, pick_x, send_x, ssem, rsem, load_sem,
):
    grp, dom = lax.axis_index("grp"), lax.axis_index("dom")
    n_grp, n_dom = lax.axis_size("grp"), lax.axis_size("dom")
    has = [dom > 0, dom < n_dom - 1, grp > 0, grp < n_grp - 1]
    peer = [(grp, dom - 1), (grp, dom + 1), (grp - 1, dom), (grp + 1, dom)]
    chunk = NB // LOADS
    loads = [
        pltpu.make_async_copy(
            state.at[:, pl.ds(q * chunk, chunk)], st.at[:, pl.ds(q * chunk, chunk)], load_sem.at[q]
        )
        for q in range(LOADS)
    ]
    for load in loads:
        load.start()
    barrier = pltpu.get_barrier_semaphore()
    for p in range(4):

        @pl.when(has[p])
        def _(p=p):
            pl.semaphore_signal(barrier, inc=1, device_id=peer[p], device_id_type=MESH)

    def build(q, carry):
        rows = pl.ds(pl.multiple_of(q * 32, 32), 32)
        for c, plane in enumerate(carried_planes(st, rows)):
            tab_c[rows, c, :] = plane
        for c in range(3):
            tab_x[rows, c, :] = st[c, rows, :]
        return carry

    for q, load in enumerate(loads):
        load.wait()
        lax.fori_loop(q * chunk // 32, (q + 1) * chunk // 32, build, 0)

    def copies(p):
        slot = p ^ 1
        return [
            pltpu.make_async_remote_copy(
                src_ref=send_c.at[pl.ds(p * HB * 8, HB * 8)],
                dst_ref=halo_c.at[pl.ds(slot * HB * 8, HB * 8)],
                send_sem=ssem.at[p, 0],
                recv_sem=rsem.at[slot, 0],
                device_id=peer[p],
                device_id_type=MESH,
            ),
            pltpu.make_async_remote_copy(
                src_ref=send_x.at[:, p],
                dst_ref=halo_x.at[:, pl.ds(slot * HB, HB)],
                send_sem=ssem.at[p, 1],
                recv_sem=rsem.at[slot, 1],
                device_id=peer[p],
                device_id_type=MESH,
            ),
        ]

    met = False
    for p in (3, 2, 1, 0):

        def pick(t, carry, p=p):
            for u in range(8):
                s = t * 8 + u
                live = jnp.where(s < counts[0, p], 1.0, 0.0).astype(F32)
                b = lists[p, s]
                send_c[pl.ds(pl.multiple_of(p * HB * 8 + s * 8, 8), 8), :] = tab_c[b] * live
                pick_x[pl.ds(pl.multiple_of(s * 8, 8), 8), :] = tab_x[b] * live
            return carry

        lax.fori_loop(0, HB // 8, pick, 0)
        for c in range(3):
            send_x[c, p] = pick_x[pl.ds(c, HB, stride=8), :]
        if not met:
            pl.semaphore_wait(barrier, sum(h.astype(jnp.int32) for h in has))
            met = True

        @pl.when(has[p])
        def _(p=p):
            for copy in copies(p):
                copy.start()

    for p in range(4):

        @pl.when(jnp.logical_not(has[p]))
        def _(p=p):
            halo_c[pl.ds(p * HB * 8, HB * 8), :] = jnp.zeros((HB * 8, 128), F32)
            halo_x[:, pl.ds(p * HB, HB), :] = jnp.zeros((3, HB, 128), F32)

    centre = [0.5 * jnp.max(st[c]) + 0.5 * jnp.min(st[c]) for c in range(3)]

    def features(source, own, first, last):
        def body(q, carry):
            rows = pl.ds(pl.multiple_of(q * 32, 32), 32)
            zero, one = jnp.zeros((32, 128), F32), jnp.ones((32, 128), F32)
            norm, xs = None, []
            for c in range(3):
                x = jnp.clip(source[c, rows, :] - centre[c], -REACH - 1.0, REACH + 1.0)
                norm = x * x if norm is None else norm + x * x
                xs.append(x)
            for c, plane in enumerate([*xs, 0.5 - norm, one, zero, zero, zero]):
                near_x[pl.ds(q * 256 + c, 32, stride=8), :] = plane
            if own:
                for c, plane in enumerate([*[2.0 * x for x in xs], one, -norm, zero, zero, zero]):
                    tab_p[pl.ds(q * 256 + c, 32, stride=8), :] = plane
            return carry

        lax.fori_loop(first // 32, last // 32, body, 0)

    def convert(own, first, last):
        def body(q, carry):
            for u in range(8):
                b = q * 8 + u
                at = pl.ds(pl.multiple_of(b * 8, 8), 8)
                n = b if own else b + NB
                x1, x2, x3 = pieces(near_x[at, :])
                feat[n] = jnp.concatenate([x1, x2, x3, x1, x2, x1], 0).astype(BF16)
                c1, c2, c3 = pieces(tab_c[b] if own else halo_c[at, :])
                car[n] = jnp.concatenate([c1, c2, c3, jnp.zeros_like(c1)], 0).astype(BF16)
                if own:
                    p1, p2, p3 = pieces(tab_p[at, :])
                    own_feat[b] = jnp.concatenate([p1, p1, p1, p2, p2, p3], 0).astype(BF16)
            return carry

        lax.fori_loop(first // 8, last // 8, body, 0)

    features(st, True, 0, NB)
    convert(True, 0, NB)
    feat[NC] = jnp.zeros((FR, 128), BF16)
    car[NC] = jnp.zeros((CR, 128), BF16)

    mv = movers[...]
    per = mv.shape[0]
    live = lax.broadcasted_iota(jnp.int32, mv.shape, 0) < mover_counts[...]
    block_of = jnp.where(live, lax.shift_right_logical(mv, 7), -1)
    lane_of = mv & 127
    gone = jnp.zeros((NB, 128), F32)
    for r in range(0, per, 2):
        b = jnp.concatenate([block_of[r : r + 1], block_of[r + 1 : r + 2]], 1)
        ln = jnp.concatenate([lane_of[r : r + 1], lane_of[r + 1 : r + 2]], 1)
        in_block = (lax.broadcasted_iota(jnp.int32, (NB, 128), 0) == b).astype(F32).astype(BF16)
        in_lane = (lax.broadcasted_iota(jnp.int32, (128, 128), 0) == ln).astype(F32).astype(BF16)
        gone = gone + lax.dot_general(in_block, in_lane, NT, preferred_element_type=F32)
    stay[...] = 1.0 - gone

    for p in range(4):

        @pl.when(has[p])
        def _(p=p):
            for copy in copies(p ^ 1):
                copy.wait_recv()

        features(halo_x, False, p * HB, p * HB + HB)
        convert(False, p * HB, p * HB + HB)

    for p in range(4):

        @pl.when(has[p])
        def _(p=p):
            for copy in copies(p):
                copy.wait_send()


def exchange(lists, counts, planes, movers, mover_counts):
    smem, vmem = pl.BlockSpec(memory_space=pltpu.SMEM), pl.BlockSpec(memory_space=pltpu.VMEM)
    return pl.pallas_call(
        exchange_kernel,
        out_shape=(
            pltpu.VMEM((3, 4 * HB, 128), F32),
            pltpu.VMEM((NC + 1, FR, 128), BF16),
            pltpu.VMEM((NB, FR, 128), BF16),
            pltpu.VMEM((NC + 1, CR, 128), BF16),
            pltpu.VMEM((NB, 128), F32),
            pltpu.VMEM((12, NB, 128), F32),
        ),
        in_specs=[smem, smem, pl.BlockSpec(memory_space=pl.ANY), vmem, vmem],
        out_specs=(vmem,) * 6,
        scratch_shapes=[
            pltpu.VMEM((4 * HB * 8, 128), F32),
            pltpu.VMEM((NB, 8, 128), F32),
            pltpu.VMEM((NB, 8, 128), F32),
            pltpu.VMEM((NB * 8, 128), F32),
            pltpu.VMEM((NB * 8, 128), F32),
            pltpu.VMEM((4 * HB * 8, 128), F32),
            pltpu.VMEM((HB * 8, 128), F32),
            pltpu.VMEM((3, 4, HB, 128), F32),
            pltpu.SemaphoreType.DMA((4, 2)),
            pltpu.SemaphoreType.DMA((4, 2)),
            pltpu.SemaphoreType.DMA((LOADS,)),
        ],
        compiler_params=pltpu.CompilerParams(
            collective_id=0, has_side_effects=True, vmem_limit_bytes=VMEM_LIMIT
        ),
    )(lists, counts, planes, movers, mover_counts)


def swap_groups(v):
    row = lax.broadcasted_iota(jnp.int32, (8, 128), 0)
    group = lax.broadcasted_iota(jnp.int32, (8, 128), 1) // 16
    apart = (row - group) & 7
    out = v
    for d in range(1, 8):
        moved = pltpu.roll(pltpu.roll(v, d, 0), 128 - 16 * d, 1)
        out = jnp.where(apart == d, moved, out)
    return out


def local_kernel(
    nbr, mask, movers_s, counts_s, st, halo_x, feat, own_feat, car, stay_ref, kept_out, message,
    tab_x, sums, upd, kept, *stages,
):
    dist, parts = stages[:RB], stages[RB:-1]
    wide = None
    for c in range(3):
        half = 0.5 * jnp.max(st[c]) - 0.5 * jnp.min(st[c])
        wide = half if wide is None else jnp.maximum(wide, half)
    close = wide <= REACH

    def slot(k, i):
        return jnp.where(mask[k, i] == 0, NC, nbr[k, i])

    def measure(p, u):
        one, two = 2 * p, 2 * p + 1
        mine = beside(own_feat[one], own_feat[two])
        for k in range(4):
            near = jnp.concatenate([feat[slot(k, one)], feat[slot(k, two)]], 0)
            dist[u][k * 128 : k * 128 + 128, :] = lax.dot_general(
                near, mine, TN, preferred_element_type=F32
            )

    def weigh(u):
        for n in range(2):
            for k in range(4):
                weights(dist[u], n * 128, k * 128, parts[u], (n * 4 + k) * 128)

    def contract(p, u):
        c = beside(*[
            jnp.concatenate([car[slot(k, i)] for k in range(4)], 1) for i in (2 * p, 2 * p + 1)
        ])
        r = jnp.dot(c, parts[u][...], preferred_element_type=F32)
        at = pl.multiple_of(p * 16, 16)
        sums[pl.ds(at, 8), :] = fold(r[0:CR])
        sums[pl.ds(at + 8, 8), :] = fold(r[CR:])

    @pl.when(close)
    def _():
        def body(t, carry):
            for u in range(U):
                p = t * U + u
                contract(jnp.maximum(p - 2, 0), (u - 2) % RB)
                weigh((u - 1) % RB)
                measure(p, u % RB)
            return carry

        lax.fori_loop(0, NB // 2 // U, body, 0)
        contract(NB // 2 - 2, RB - 2)
        weigh(RB - 1)
        contract(NB // 2 - 1, RB - 1)

    @pl.when(jnp.logical_not(close))
    def _():
        def raw(q, carry):
            own = pl.ds(pl.multiple_of(q * 32, 32), 32)
            for c in range(3):
                tab_x[pl.ds(q * 256 + c, 32, stride=8), :] = st[c, own, :]
                tab_x[pl.ds(NB * 8 + q * 256 + c, 32, stride=8), :] = halo_x[c, own, :]
            return carry

        lax.fori_loop(0, NB // 32, raw, 0)

        def body(i, carry):
            columns = jnp.transpose(tab_x[pl.ds(pl.multiple_of(i * 8, 8), 8), :])

            def pair(k, total):
                near = tab_x[pl.ds(pl.multiple_of(nbr[k, i] * 8, 8), 8), :]
                s = jnp.full((128, 128), 0.5, F32)
                for c in range(3):
                    delta = columns[:, c : c + 1] - near[c : c + 1, :]
                    s = s - delta * delta
                s = jnp.maximum(s, 0.0)
                h, rest = split(s * s * s)
                cc = car[slot(k, i)]
                return total + lax.dot_general(cc, jnp.concatenate([h, rest], 0), NT, preferred_element_type=F32)

            total = lax.fori_loop(0, 4, pair, jnp.zeros((CR, 256), F32))
            sums[pl.ds(pl.multiple_of(i * 8, 8), 8), :] = fold(total)
            return carry

        lax.fori_loop(0, NB, body, 0)

    def advance(q, carry):
        rows = pl.ds(pl.multiple_of(q * 32, 32), 32)
        total = [8.0 * sums[pl.ds(q * 256 + c, 32, stride=8), :] for c in range(8)]
        position = [st[c, rows, :] for c in range(3)]
        velocity = [st[3 + c, rows, :] for c in range(3)]
        temper, one, two, solid = (st[c, rows, :] for c in range(8, 12))
        vol = total[1]
        temp_one = temper + 0.25 * (total[2] - temper * vol)
        conc_one = one + 0.2 * (total[3] - one * vol)
        conc_two = two + 0.1 * (total[4] - two * vol)
        v_new = [velocity[c] + 0.3 * (total[5 + c] - velocity[c] * vol) for c in range(3)]
        x_new = [position[c] + 0.02 * v_new[c] for c in range(3)]
        liquidus = 1.0 - 0.3 * conc_one - 0.2 * conc_two
        solid_new = jnp.maximum(solid, jnp.clip(2.0 * (liquidus - temp_one), 0.0, 1.0))
        temp_two = temp_one + 0.4 * (solid_new - solid)
        one_new = conc_one * (1.0 - 0.83 * solid) / (1.0 - 0.83 * solid_new)
        two_new = conc_two * (1.0 - 0.6 * solid) / (1.0 - 0.6 * solid_new)
        updated = [*x_new, *v_new, st[6, rows, :], total[0], temp_two, one_new, two_new, solid_new]
        stay = stay_ref[rows, :]
        for c, plane in enumerate(updated):
            kept[c, rows, :] = plane * stay
            upd[pl.ds(q * 512 + c, 32, stride=16), :] = plane
        zero = jnp.zeros((32, 128), F32)
        for c in range(12, 16):
            upd[pl.ds(q * 512 + c, 32, stride=16), :] = zero
        return carry

    lax.fori_loop(0, NB // 32, advance, 0)

    out_copy = pltpu.make_async_copy(kept, kept_out, stages[-1])
    out_copy.start()
    lane = lax.broadcasted_iota(jnp.int32, (16, 128), 1)

    def gather(g, carry):
        def to(z):
            return (g // 2) * 16 + 2 * z + g % 2

        count = jnp.zeros((16, 128), jnp.int32)
        for q in range(8):
            count = jnp.where(lax.shift_right_logical(lane, 4) == q, counts_s[0, to(q)], count)
        acc = jnp.zeros((16, 128), F32)
        for t in range(128):
            m = movers_s[t % 16, to(t // 16)]
            at = pl.multiple_of(lax.shift_right_logical(m, 7) * 16, 16)
            acc = jnp.where(lane == t, pltpu.roll(upd[pl.ds(at, 16), :], (t - m) & 127, 1), acc)
        acc = jnp.where((lane & 15) < count, acc, 0.0)
        for h in range(2):
            message[pl.ds(g * 16 + h, 8, stride=2), :] = swap_groups(acc[8 * h : 8 * h + 8])
        return carry

    lax.fori_loop(0, movers_s.shape[1] // 8, gather, 0)
    out_copy.wait()


def local_step(nbr, mask, movers, counts, planes, tables):
    smem, vmem = pl.BlockSpec(memory_space=pltpu.SMEM), pl.BlockSpec(memory_space=pltpu.VMEM)
    doms = movers.shape[1]
    return pl.pallas_call(
        local_kernel,
        out_shape=(
            pltpu.HBM((12, NB, 128), F32),
            pltpu.VMEM((2 * doms, 128), F32),
        ),
        in_specs=[smem] * 4 + [vmem] * 6,
        out_specs=(pl.BlockSpec(memory_space=pl.ANY), vmem),
        scratch_shapes=[
            pltpu.VMEM((NC * 8, 128), F32),
            pltpu.VMEM((NB * 8, 128), F32),
            pltpu.VMEM((NB * 16, 128), F32),
            pltpu.VMEM((12, NB, 128), F32),
            *[pltpu.VMEM((512, 256), F32)] * RB,
            *[pltpu.VMEM((1024, 256), BF16)] * RB,
            pltpu.SemaphoreType.DMA,
        ],
        compiler_params=pltpu.CompilerParams(vmem_limit_bytes=VMEM_LIMIT),
    )(nbr, mask, movers, counts, pltpu.with_memory_space_constraint(planes, pltpu.VMEM), *[pltpu.with_memory_space_constraint(t, pltpu.VMEM) for t in tables])


def migrate_kernel(message, out, first, landed, ssem, rsem):
    grp, me = lax.axis_index("grp"), lax.axis_index("dom")
    y, z, core = me // 16, lax.rem(me // 2, 8), lax.rem(me, 2)
    place = y * 2 + core

    def across(k):
        other = lax.rem(place + k, 8)
        return other // 2, z, lax.rem(other, 2)

    def along(k):
        return y, lax.rem(z + k, 8), core

    def device(at):
        return (grp, at[0] * 16 + at[1] * 2 + at[2])

    barrier = pltpu.get_barrier_semaphore()
    for k in range(1, 8):
        for at in (across(k), along(k)):
            pl.semaphore_signal(barrier, inc=1, device_id=device(at), device_id_type=MESH)
    first[place] = message[place]
    pl.semaphore_wait(barrier, 14)

    def hop_one(k):
        at = across(k)
        return pltpu.make_async_remote_copy(
            src_ref=message.at[at[0] * 2 + at[2]],
            dst_ref=first.at[place],
            send_sem=ssem.at[0, k],
            recv_sem=rsem.at[0, k],
            device_id=device(at),
            device_id_type=MESH,
        )

    def hop_two(k):
        at = along(k)
        return pltpu.make_async_remote_copy(
            src_ref=first.at[:, at[1]],
            dst_ref=landed.at[z],
            send_sem=ssem.at[1, k],
            recv_sem=rsem.at[1, k],
            device_id=device(at),
            device_id_type=MESH,
        )

    one, two = [hop_one(k) for k in range(1, 8)], [hop_two(k) for k in range(1, 8)]
    for copy in one:
        copy.start()
    for copy in one:
        copy.wait_recv()
    for copy in two:
        copy.start()
    landed[z] = first[:, z]
    for copy in one:
        copy.wait_send()
    for copy in two:
        copy.wait()
    for g in range(8):
        for h in range(2):
            v = landed[pl.ds((g % 2) * 4, 4), pl.ds((g // 2) * 2, 2), h, :].reshape(8, 128)
            rows = 8 if h == 0 else 4
            out[8 * h : 8 * h + rows, g * 128 : g * 128 + 128] = swap_groups(v)[:rows]


def migrate(message):
    vmem = pl.BlockSpec(memory_space=pltpu.VMEM)
    return pl.pallas_call(
        migrate_kernel,
        out_shape=jax.ShapeDtypeStruct((12, 1024), F32),
        in_specs=[vmem],
        out_specs=vmem,
        scratch_shapes=[
            pltpu.VMEM((8, 8, 2, 128), F32),
            pltpu.VMEM((8, 8, 2, 128), F32),
            pltpu.SemaphoreType.DMA((2, 8)),
            pltpu.SemaphoreType.DMA((2, 8)),
        ],
        compiler_params=pltpu.CompilerParams(
            collective_id=1, has_side_effects=True, vmem_limit_bytes=VMEM_LIMIT
        ),
    )(pltpu.with_memory_space_constraint(message, pltpu.VMEM))


def on_device(state, neighbours, pair_mask, send_lists, send_counts, movers, mover_counts):
    def far(x):
        return pltpu.with_memory_space_constraint(x, pltpu.HBM)

    planes = far(state.transpose(1, 0, 2))
    slots, counts = far(movers[0].T), far(mover_counts)
    *tables, planes = exchange(far(send_lists[0]), far(send_counts), planes, slots, counts)
    kept, message = local_step(far(neighbours.T), far(pair_mask.T), slots, counts, planes, tables)
    arrivals = migrate(message.reshape(8, 8, 2, 128))
    return kept.transpose(1, 0, 2), arrivals


def solution(mesh):
    both = ("grp", "dom")
    placed = (P(both, None, None), P(both, None), P(both, None), P(both, None, None), P(both, None), P(both, None, None), P(both, None))
    return jax.shard_map(
        on_device,
        mesh=mesh,
        in_specs=placed,
        out_specs=(P(both, None, None), P(None, both)),
        check_vma=False,
    )
```

```python
import jax
import jax.numpy as jnp
from jax import lax
from jax.experimental import pallas as pl
from jax.experimental.pallas import tpu as pltpu
from jax.sharding import PartitionSpec as P

MESH = pl.DeviceIdType.MESH
F32 = jnp.float32
BF16 = jnp.bfloat16
NB = 256
HB = 64
NC = 512
FR = 48
CR = 32
U = 32
RB = 4
LOADS = 4
REACH = 2.0
NT = (((1,), (1,)), ((), ()))
TN = (((0,), (0,)), ((), ()))
VMEM_LIMIT = 40 << 20


def carried_planes(st, rows):
    mass = st[6, rows, :]
    volume = mass / st[7, rows, :]
    out = [mass, volume]
    for ch in (8, 9, 10, 3, 4, 5):
        out.append(volume * st[ch, rows, :])
    return out


def split(w):
    h = w.astype(BF16)
    return h, (w - h.astype(F32)).astype(BF16)


def weights(dist, lane, row, parts, out_row):
    s = jnp.maximum(dist[row : row + 128, lane : lane + 128], 0.0)
    h, rest = split(s * s * s)
    parts[out_row : out_row + 128, 0:128] = h
    parts[out_row : out_row + 128, 128:256] = rest


def beside(one, two):
    return jnp.concatenate(
        [
            jnp.concatenate([one, jnp.zeros_like(two)], 1),
            jnp.concatenate([jnp.zeros_like(one), two], 1),
        ],
        0,
    )


def fold(r):
    r = r[:, 0:128] + r[:, 128:256]
    return r[0:8] + r[8:16] + r[16:24]


def pieces(v):
    first = v.astype(BF16).astype(F32)
    rest = v - first
    second = rest.astype(BF16).astype(F32)
    return first, second, rest - second


def exchange_kernel(
    lists, counts, state, movers, mover_counts, halo_x, feat, own_feat, car, stay, st,
    halo_c, tab_c, tab_x, near_x, tab_p, send_c, pick_x, send_x, ssem, rsem, load_sem,
):
    grp, dom = lax.axis_index("grp"), lax.axis_index("dom")
    n_grp, n_dom = lax.axis_size("grp"), lax.axis_size("dom")
    has = [dom > 0, dom < n_dom - 1, grp > 0, grp < n_grp - 1]
    peer = [(grp, dom - 1), (grp, dom + 1), (grp - 1, dom), (grp + 1, dom)]
    chunk = NB // LOADS
    loads = [
        pltpu.make_async_copy(
            state.at[:, pl.ds(q * chunk, chunk)], st.at[:, pl.ds(q * chunk, chunk)], load_sem.at[q]
        )
        for q in range(LOADS)
    ]
    for load in loads:
        load.start()
    barrier = pltpu.get_barrier_semaphore()
    for p in range(4):

        @pl.when(has[p])
        def _(p=p):
            pl.semaphore_signal(barrier, inc=1, device_id=peer[p], device_id_type=MESH)

    def build(q, carry):
        rows = pl.ds(pl.multiple_of(q * 32, 32), 32)
        for c, plane in enumerate(carried_planes(st, rows)):
            tab_c[rows, c, :] = plane
        for c in range(3):
            tab_x[rows, c, :] = st[c, rows, :]
        return carry

    for q, load in enumerate(loads):
        load.wait()
        lax.fori_loop(q * chunk // 32, (q + 1) * chunk // 32, build, 0)

    def copies(p):
        slot = p ^ 1
        return [
            pltpu.make_async_remote_copy(
                src_ref=send_c.at[pl.ds(p * HB * 8, HB * 8)],
                dst_ref=halo_c.at[pl.ds(slot * HB * 8, HB * 8)],
                send_sem=ssem.at[p, 0],
                recv_sem=rsem.at[slot, 0],
                device_id=peer[p],
                device_id_type=MESH,
            ),
            pltpu.make_async_remote_copy(
                src_ref=send_x.at[:, p],
                dst_ref=halo_x.at[:, pl.ds(slot * HB, HB)],
                send_sem=ssem.at[p, 1],
                recv_sem=rsem.at[slot, 1],
                device_id=peer[p],
                device_id_type=MESH,
            ),
        ]

    met = False
    for p in (3, 2, 1, 0):

        def pick(t, carry, p=p):
            for u in range(8):
                s = t * 8 + u
                live = jnp.where(s < counts[0, p], 1.0, 0.0).astype(F32)
                b = lists[p, s]
                send_c[pl.ds(pl.multiple_of(p * HB * 8 + s * 8, 8), 8), :] = tab_c[b] * live
                pick_x[pl.ds(pl.multiple_of(s * 8, 8), 8), :] = tab_x[b] * live
            return carry

        lax.fori_loop(0, HB // 8, pick, 0)
        for c in range(3):
            send_x[c, p] = pick_x[pl.ds(c, HB, stride=8), :]
        if not met:
            pl.semaphore_wait(barrier, sum(h.astype(jnp.int32) for h in has))
            met = True

        @pl.when(has[p])
        def _(p=p):
            for copy in copies(p):
                copy.start()

    for p in range(4):

        @pl.when(jnp.logical_not(has[p]))
        def _(p=p):
            halo_c[pl.ds(p * HB * 8, HB * 8), :] = jnp.zeros((HB * 8, 128), F32)
            halo_x[:, pl.ds(p * HB, HB), :] = jnp.zeros((3, HB, 128), F32)

    centre = [0.5 * jnp.max(st[c]) + 0.5 * jnp.min(st[c]) for c in range(3)]

    def features(source, own, first, last):
        def body(q, carry):
            rows = pl.ds(pl.multiple_of(q * 32, 32), 32)
            zero, one = jnp.zeros((32, 128), F32), jnp.ones((32, 128), F32)
            norm, xs = None, []
            for c in range(3):
                x = jnp.clip(source[c, rows, :] - centre[c], -REACH - 1.0, REACH + 1.0)
                norm = x * x if norm is None else norm + x * x
                xs.append(x)
            for c, plane in enumerate([*xs, 0.5 - norm, one, zero, zero, zero]):
                near_x[pl.ds(q * 256 + c, 32, stride=8), :] = plane
            if own:
                for c, plane in enumerate([*[2.0 * x for x in xs], one, -norm, zero, zero, zero]):
                    tab_p[pl.ds(q * 256 + c, 32, stride=8), :] = plane
            return carry

        lax.fori_loop(first // 32, last // 32, body, 0)

    def convert(own, first, last):
        def body(q, carry):
            for u in range(8):
                b = q * 8 + u
                at = pl.ds(pl.multiple_of(b * 8, 8), 8)
                n = b if own else b + NB
                x1, x2, x3 = pieces(near_x[at, :])
                feat[n] = jnp.concatenate([x1, x2, x3, x1, x2, x1], 0).astype(BF16)
                c1, c2, c3 = pieces(tab_c[b] if own else halo_c[at, :])
                car[n] = jnp.concatenate([c1, c2, c3, jnp.zeros_like(c1)], 0).astype(BF16)
                if own:
                    p1, p2, p3 = pieces(tab_p[at, :])
                    own_feat[b] = jnp.concatenate([p1, p1, p1, p2, p2, p3], 0).astype(BF16)
            return carry

        lax.fori_loop(first // 8, last // 8, body, 0)

    features(st, True, 0, NB)
    convert(True, 0, NB)
    feat[NC] = jnp.zeros((FR, 128), BF16)
    car[NC] = jnp.zeros((CR, 128), BF16)

    mv = movers[...]
    per = mv.shape[0]
    live = lax.broadcasted_iota(jnp.int32, mv.shape, 0) < mover_counts[...]
    block_of = jnp.where(live, lax.shift_right_logical(mv, 7), -1)
    lane_of = mv & 127
    gone = jnp.zeros((NB, 128), F32)
    for r in range(0, per, 2):
        b = jnp.concatenate([block_of[r : r + 1], block_of[r + 1 : r + 2]], 1)
        ln = jnp.concatenate([lane_of[r : r + 1], lane_of[r + 1 : r + 2]], 1)
        in_block = (lax.broadcasted_iota(jnp.int32, (NB, 128), 0) == b).astype(F32).astype(BF16)
        in_lane = (lax.broadcasted_iota(jnp.int32, (128, 128), 0) == ln).astype(F32).astype(BF16)
        gone = gone + lax.dot_general(in_block, in_lane, NT, preferred_element_type=F32)
    stay[...] = 1.0 - gone

    for p in range(4):

        @pl.when(has[p])
        def _(p=p):
            for copy in copies(p ^ 1):
                copy.wait_recv()

        features(halo_x, False, p * HB, p * HB + HB)
        convert(False, p * HB, p * HB + HB)

    for p in range(4):

        @pl.when(has[p])
        def _(p=p):
            for copy in copies(p):
                copy.wait_send()


def exchange(lists, counts, planes, movers, mover_counts):
    smem, vmem = pl.BlockSpec(memory_space=pltpu.SMEM), pl.BlockSpec(memory_space=pltpu.VMEM)
    return pl.pallas_call(
        exchange_kernel,
        out_shape=(
            pltpu.VMEM((3, 4 * HB, 128), F32),
            pltpu.VMEM((NC + 1, FR, 128), BF16),
            pltpu.VMEM((NB, FR, 128), BF16),
            pltpu.VMEM((NC + 1, CR, 128), BF16),
            pltpu.VMEM((NB, 128), F32),
            pltpu.VMEM((12, NB, 128), F32),
        ),
        in_specs=[smem, smem, pl.BlockSpec(memory_space=pl.ANY), vmem, vmem],
        out_specs=(vmem,) * 6,
        scratch_shapes=[
            pltpu.VMEM((4 * HB * 8, 128), F32),
            pltpu.VMEM((NB, 8, 128), F32),
            pltpu.VMEM((NB, 8, 128), F32),
            pltpu.VMEM((NB * 8, 128), F32),
            pltpu.VMEM((NB * 8, 128), F32),
            pltpu.VMEM((4 * HB * 8, 128), F32),
            pltpu.VMEM((HB * 8, 128), F32),
            pltpu.VMEM((3, 4, HB, 128), F32),
            pltpu.SemaphoreType.DMA((4, 2)),
            pltpu.SemaphoreType.DMA((4, 2)),
            pltpu.SemaphoreType.DMA((LOADS,)),
        ],
        compiler_params=pltpu.CompilerParams(
            collective_id=0, has_side_effects=True, vmem_limit_bytes=VMEM_LIMIT
        ),
    )(lists, counts, planes, movers, mover_counts)


def swap_groups(v):
    row = lax.broadcasted_iota(jnp.int32, (8, 128), 0)
    group = lax.broadcasted_iota(jnp.int32, (8, 128), 1) // 16
    apart = (row - group) & 7
    out = v
    for d in range(1, 8):
        moved = pltpu.roll(pltpu.roll(v, d, 0), 128 - 16 * d, 1)
        out = jnp.where(apart == d, moved, out)
    return out


def local_kernel(
    nbr, mask, st, halo_x, feat, own_feat, car, stay_ref, kept_out, upd,
    tab_x, sums, kept, out_sem, *stages,
):
    dist, parts = stages[:RB], stages[RB:]
    wide = None
    for c in range(3):
        half = 0.5 * jnp.max(st[c]) - 0.5 * jnp.min(st[c])
        wide = half if wide is None else jnp.maximum(wide, half)
    close = wide <= REACH

    def slot(k, i):
        return jnp.where(mask[k, i] == 0, NC, nbr[k, i])

    def measure(p, u):
        one, two = 2 * p, 2 * p + 1
        mine = beside(own_feat[one], own_feat[two])
        for k in range(4):
            near = jnp.concatenate([feat[slot(k, one)], feat[slot(k, two)]], 0)
            dist[u][k * 128 : k * 128 + 128, :] = lax.dot_general(
                near, mine, TN, preferred_element_type=F32
            )

    def weigh(u):
        for n in range(2):
            for k in range(4):
                weights(dist[u], n * 128, k * 128, parts[u], (n * 4 + k) * 128)

    def contract(p, u):
        c = beside(*[
            jnp.concatenate([car[slot(k, i)] for k in range(4)], 1) for i in (2 * p, 2 * p + 1)
        ])
        r = jnp.dot(c, parts[u][...], preferred_element_type=F32)
        at = pl.multiple_of(p * 16, 16)
        sums[pl.ds(at, 8), :] = fold(r[0:CR])
        sums[pl.ds(at + 8, 8), :] = fold(r[CR:])

    @pl.when(close)
    def _():
        def body(t, carry):
            for u in range(U):
                p = t * U + u
                contract(jnp.maximum(p - 2, 0), (u - 2) % RB)
                weigh((u - 1) % RB)
                measure(p, u % RB)
            return carry

        lax.fori_loop(0, NB // 2 // U, body, 0)
        contract(NB // 2 - 2, RB - 2)
        weigh(RB - 1)
        contract(NB // 2 - 1, RB - 1)

    @pl.when(jnp.logical_not(close))
    def _():
        def raw(q, carry):
            own = pl.ds(pl.multiple_of(q * 32, 32), 32)
            for c in range(3):
                tab_x[pl.ds(q * 256 + c, 32, stride=8), :] = st[c, own, :]
                tab_x[pl.ds(NB * 8 + q * 256 + c, 32, stride=8), :] = halo_x[c, own, :]
            return carry

        lax.fori_loop(0, NB // 32, raw, 0)

        def body(i, carry):
            columns = jnp.transpose(tab_x[pl.ds(pl.multiple_of(i * 8, 8), 8), :])

            def pair(k, total):
                near = tab_x[pl.ds(pl.multiple_of(nbr[k, i] * 8, 8), 8), :]
                s = jnp.full((128, 128), 0.5, F32)
                for c in range(3):
                    delta = columns[:, c : c + 1] - near[c : c + 1, :]
                    s = s - delta * delta
                s = jnp.maximum(s, 0.0)
                h, rest = split(s * s * s)
                cc = car[slot(k, i)]
                return total + lax.dot_general(cc, jnp.concatenate([h, rest], 0), NT, preferred_element_type=F32)

            total = lax.fori_loop(0, 4, pair, jnp.zeros((CR, 256), F32))
            sums[pl.ds(pl.multiple_of(i * 8, 8), 8), :] = fold(total)
            return carry

        lax.fori_loop(0, NB, body, 0)

    def advance(q, carry):
        rows = pl.ds(pl.multiple_of(q * 32, 32), 32)
        total = [8.0 * sums[pl.ds(q * 256 + c, 32, stride=8), :] for c in range(8)]
        position = [st[c, rows, :] for c in range(3)]
        velocity = [st[3 + c, rows, :] for c in range(3)]
        temper, one, two, solid = (st[c, rows, :] for c in range(8, 12))
        vol = total[1]
        temp_one = temper + 0.25 * (total[2] - temper * vol)
        conc_one = one + 0.2 * (total[3] - one * vol)
        conc_two = two + 0.1 * (total[4] - two * vol)
        v_new = [velocity[c] + 0.3 * (total[5 + c] - velocity[c] * vol) for c in range(3)]
        x_new = [position[c] + 0.02 * v_new[c] for c in range(3)]
        liquidus = 1.0 - 0.3 * conc_one - 0.2 * conc_two
        solid_new = jnp.maximum(solid, jnp.clip(2.0 * (liquidus - temp_one), 0.0, 1.0))
        temp_two = temp_one + 0.4 * (solid_new - solid)
        one_new = conc_one * (1.0 - 0.83 * solid) / (1.0 - 0.83 * solid_new)
        two_new = conc_two * (1.0 - 0.6 * solid) / (1.0 - 0.6 * solid_new)
        updated = [*x_new, *v_new, st[6, rows, :], total[0], temp_two, one_new, two_new, solid_new]
        stay = stay_ref[rows, :]
        for c, plane in enumerate(updated):
            kept[c, rows, :] = plane * stay
            upd[rows, c, :] = plane
        zero = jnp.zeros((32, 128), F32)
        for c in range(12, 16):
            upd[rows, c, :] = zero
        leave(q).start()
        return carry

    def leave(q):
        rows = pl.ds(pl.multiple_of(q * 32, 32), 32)
        return pltpu.make_async_copy(kept.at[:, rows], kept_out.at[:, rows], out_sem.at[q])

    lax.fori_loop(0, NB // 32, advance, 0)
    for q in range(NB // 32):
        leave(q).wait()


def local_step(nbr, mask, planes, tables):
    smem, vmem = pl.BlockSpec(memory_space=pltpu.SMEM), pl.BlockSpec(memory_space=pltpu.VMEM)
    return pl.pallas_call(
        local_kernel,
        out_shape=(
            pltpu.HBM((12, NB, 128), F32),
            pltpu.VMEM((NB, 16, 128), F32),
        ),
        in_specs=[smem] * 2 + [vmem] * 6,
        out_specs=(pl.BlockSpec(memory_space=pl.ANY), vmem),
        scratch_shapes=[
            pltpu.VMEM((NC * 8, 128), F32),
            pltpu.VMEM((NB * 8, 128), F32),
            pltpu.VMEM((12, NB, 128), F32),
            pltpu.SemaphoreType.DMA((NB // 32,)),
            *[pltpu.VMEM((512, 256), F32)] * RB,
            *[pltpu.VMEM((1024, 256), BF16)] * RB,
        ],
        compiler_params=pltpu.CompilerParams(vmem_limit_bytes=VMEM_LIMIT),
    )(nbr, mask, pltpu.with_memory_space_constraint(planes, pltpu.VMEM), *[pltpu.with_memory_space_constraint(t, pltpu.VMEM) for t in tables])


def migrate_kernel(movers_s, counts_s, upd, out, message, first, landed, ssem, rsem):
    grp, me = lax.axis_index("grp"), lax.axis_index("dom")
    y, z, core = me // 16, lax.rem(me // 2, 8), lax.rem(me, 2)
    place = y * 2 + core

    def across(k):
        other = lax.rem(place + k, 8)
        return other // 2, z, lax.rem(other, 2)

    def along(k):
        return y, lax.rem(z + k, 8), core

    def device(at):
        return (grp, at[0] * 16 + at[1] * 2 + at[2])

    barrier = pltpu.get_barrier_semaphore()
    for k in range(1, 8):
        for at in (across(k), along(k)):
            pl.semaphore_signal(barrier, inc=1, device_id=device(at), device_id_type=MESH)

    lane = lax.broadcasted_iota(jnp.int32, (16, 128), 1)

    def gather(g, carry):
        def to(z):
            return (g // 2) * 16 + 2 * z + g % 2

        count = jnp.zeros((16, 128), jnp.int32)
        for q in range(8):
            count = jnp.where(lax.shift_right_logical(lane, 4) == q, counts_s[0, to(q)], count)
        acc = jnp.zeros((16, 128), F32)
        for t in range(128):
            m = movers_s[t % 16, to(t // 16)]
            acc = jnp.where(lane == t, pltpu.roll(upd[lax.shift_right_logical(m, 7)], (t - m) & 127, 1), acc)
        acc = jnp.where((lane & 15) < count, acc, 0.0)
        for h in range(2):
            message[g, :, h, :] = swap_groups(acc[8 * h : 8 * h + 8])
        return carry

    lax.fori_loop(0, 8, gather, 0)
    first[place] = message[place]
    pl.semaphore_wait(barrier, 14)

    def hop_one(k):
        at = across(k)
        return pltpu.make_async_remote_copy(
            src_ref=message.at[at[0] * 2 + at[2]],
            dst_ref=first.at[place],
            send_sem=ssem.at[0, k],
            recv_sem=rsem.at[0, k],
            device_id=device(at),
            device_id_type=MESH,
        )

    def hop_two(k):
        at = along(k)
        return pltpu.make_async_remote_copy(
            src_ref=first.at[:, at[1]],
            dst_ref=landed.at[z],
            send_sem=ssem.at[1, k],
            recv_sem=rsem.at[1, k],
            device_id=device(at),
            device_id_type=MESH,
        )

    one, two = [hop_one(k) for k in range(1, 8)], [hop_two(k) for k in range(1, 8)]
    for copy in one:
        copy.start()
    for copy in one:
        copy.wait_recv()
    for copy in two:
        copy.start()
    landed[z] = first[:, z]
    for copy in one:
        copy.wait_send()
    for copy in two:
        copy.wait()
    for g in range(8):
        for h in range(2):
            v = landed[pl.ds((g % 2) * 4, 4), pl.ds((g // 2) * 2, 2), h, :].reshape(8, 128)
            rows = 8 if h == 0 else 4
            out[8 * h : 8 * h + rows, g * 128 : g * 128 + 128] = swap_groups(v)[:rows]


def migrate(movers, counts, upd):
    smem, vmem = pl.BlockSpec(memory_space=pltpu.SMEM), pl.BlockSpec(memory_space=pltpu.VMEM)
    return pl.pallas_call(
        migrate_kernel,
        out_shape=jax.ShapeDtypeStruct((12, 1024), F32),
        in_specs=[smem, smem, vmem],
        out_specs=vmem,
        scratch_shapes=[
            pltpu.VMEM((8, 8, 2, 128), F32),
            pltpu.VMEM((8, 8, 2, 128), F32),
            pltpu.VMEM((8, 8, 2, 128), F32),
            pltpu.SemaphoreType.DMA((2, 8)),
            pltpu.SemaphoreType.DMA((2, 8)),
        ],
        compiler_params=pltpu.CompilerParams(
            collective_id=1, has_side_effects=True, vmem_limit_bytes=VMEM_LIMIT
        ),
    )(movers, counts, pltpu.with_memory_space_constraint(upd, pltpu.VMEM))


def on_device(state, neighbours, pair_mask, send_lists, send_counts, movers, mover_counts):
    def far(x):
        return pltpu.with_memory_space_constraint(x, pltpu.HBM)

    planes = far(state.transpose(1, 0, 2))
    slots, counts = far(movers[0].T), far(mover_counts)
    *tables, planes = exchange(far(send_lists[0]), far(send_counts), planes, slots, counts)
    kept, upd = local_step(far(neighbours.T), far(pair_mask.T), planes, tables)
    arrivals = migrate(slots, counts, upd)
    return kept.transpose(1, 0, 2), arrivals


def solution(mesh):
    both = ("grp", "dom")
    placed = (P(both, None, None), P(both, None), P(both, None), P(both, None, None), P(both, None), P(both, None, None), P(both, None))
    return jax.shard_map(
        on_device,
        mesh=mesh,
        in_specs=placed,
        out_specs=(P(both, None, None), P(None, both)),
        check_vma=False,
    )
```

```python
import jax
import jax.numpy as jnp
from jax import lax
from jax.experimental import pallas as pl
from jax.experimental.pallas import tpu as pltpu
from jax.sharding import PartitionSpec as P

MESH = pl.DeviceIdType.MESH
F32 = jnp.float32
BF16 = jnp.bfloat16
NB = 256
HB = 64
NC = 512
FR = 48
CR = 32
U = 64
RB = 4
LOADS = 4
REACH = 2.0
NT = (((1,), (1,)), ((), ()))
TN = (((0,), (0,)), ((), ()))
VMEM_LIMIT = 40 << 20


def carried_planes(st, rows):
    mass = st[6, rows, :]
    volume = mass / st[7, rows, :]
    out = [mass, volume]
    for ch in (8, 9, 10, 3, 4, 5):
        out.append(volume * st[ch, rows, :])
    return out


def split(w):
    h = w.astype(BF16)
    return h, (w - h.astype(F32)).astype(BF16)


def weights(dist, lane, row, parts, out_row):
    s = jnp.maximum(dist[row : row + 128, lane : lane + 128], 0.0)
    h, rest = split(s * s * s)
    parts[out_row : out_row + 128, 0:128] = h
    parts[out_row : out_row + 128, 128:256] = rest


def beside(one, two):
    return jnp.concatenate(
        [
            jnp.concatenate([one, jnp.zeros_like(two)], 1),
            jnp.concatenate([jnp.zeros_like(one), two], 1),
        ],
        0,
    )


def fold(r):
    r = r[:, 0:128] + r[:, 128:256]
    return r[0:8] + r[8:16] + r[16:24]


def pieces(v):
    first = v.astype(BF16).astype(F32)
    rest = v - first
    second = rest.astype(BF16).astype(F32)
    return first, second, rest - second


def exchange_kernel(
    lists, counts, state, movers, mover_counts, halo_x, feat, own_feat, car, stay, st,
    halo_c, tab_c, tab_x, near_x, tab_p, send_c, pick_x, send_x, ssem, rsem, load_sem,
):
    grp, dom = lax.axis_index("grp"), lax.axis_index("dom")
    n_grp, n_dom = lax.axis_size("grp"), lax.axis_size("dom")
    has = [dom > 0, dom < n_dom - 1, grp > 0, grp < n_grp - 1]
    peer = [(grp, dom - 1), (grp, dom + 1), (grp - 1, dom), (grp + 1, dom)]
    chunk = NB // LOADS
    loads = [
        pltpu.make_async_copy(
            state.at[:, pl.ds(q * chunk, chunk)], st.at[:, pl.ds(q * chunk, chunk)], load_sem.at[q]
        )
        for q in range(LOADS)
    ]
    for load in loads:
        load.start()
    barrier = pltpu.get_barrier_semaphore()
    for p in range(4):

        @pl.when(has[p])
        def _(p=p):
            pl.semaphore_signal(barrier, inc=1, device_id=peer[p], device_id_type=MESH)

    def build(q, carry):
        rows = pl.ds(pl.multiple_of(q * 32, 32), 32)
        for c, plane in enumerate(carried_planes(st, rows)):
            tab_c[rows, c, :] = plane
        for c in range(3):
            tab_x[rows, c, :] = st[c, rows, :]
        return carry

    for q, load in enumerate(loads):
        load.wait()
        lax.fori_loop(q * chunk // 32, (q + 1) * chunk // 32, build, 0)

    def copies(p):
        slot = p ^ 1
        return [
            pltpu.make_async_remote_copy(
                src_ref=send_c.at[pl.ds(p * HB * 8, HB * 8)],
                dst_ref=halo_c.at[pl.ds(slot * HB * 8, HB * 8)],
                send_sem=ssem.at[p, 0],
                recv_sem=rsem.at[slot, 0],
                device_id=peer[p],
                device_id_type=MESH,
            ),
            pltpu.make_async_remote_copy(
                src_ref=send_x.at[:, p],
                dst_ref=halo_x.at[:, pl.ds(slot * HB, HB)],
                send_sem=ssem.at[p, 1],
                recv_sem=rsem.at[slot, 1],
                device_id=peer[p],
                device_id_type=MESH,
            ),
        ]

    met = False
    for p in (3, 2, 1, 0):

        def pick(t, carry, p=p):
            for u in range(8):
                s = t * 8 + u
                live = jnp.where(s < counts[0, p], 1.0, 0.0).astype(F32)
                b = lists[p, s]
                send_c[pl.ds(pl.multiple_of(p * HB * 8 + s * 8, 8), 8), :] = tab_c[b] * live
                pick_x[pl.ds(pl.multiple_of(s * 8, 8), 8), :] = tab_x[b] * live
            return carry

        lax.fori_loop(0, HB // 8, pick, 0)
        for c in range(3):
            send_x[c, p] = pick_x[pl.ds(c, HB, stride=8), :]
        if not met:
            pl.semaphore_wait(barrier, sum(h.astype(jnp.int32) for h in has))
            met = True

        @pl.when(has[p])
        def _(p=p):
            for copy in copies(p):
                copy.start()

    for p in range(4):

        @pl.when(jnp.logical_not(has[p]))
        def _(p=p):
            halo_c[pl.ds(p * HB * 8, HB * 8), :] = jnp.zeros((HB * 8, 128), F32)
            halo_x[:, pl.ds(p * HB, HB), :] = jnp.zeros((3, HB, 128), F32)

    centre = [0.5 * jnp.max(st[c]) + 0.5 * jnp.min(st[c]) for c in range(3)]

    def features(source, own, first, last):
        def body(q, carry):
            rows = pl.ds(pl.multiple_of(q * 32, 32), 32)
            zero, one = jnp.zeros((32, 128), F32), jnp.ones((32, 128), F32)
            norm, xs = None, []
            for c in range(3):
                x = jnp.clip(source[c, rows, :] - centre[c], -REACH - 1.0, REACH + 1.0)
                norm = x * x if norm is None else norm + x * x
                xs.append(x)
            for c, plane in enumerate([*xs, 0.5 - norm, one, zero, zero, zero]):
                near_x[pl.ds(q * 256 + c, 32, stride=8), :] = plane
            if own:
                for c, plane in enumerate([*[2.0 * x for x in xs], one, -norm, zero, zero, zero]):
                    tab_p[pl.ds(q * 256 + c, 32, stride=8), :] = plane
            return carry

        lax.fori_loop(first // 32, last // 32, body, 0)

    def convert(own, first, last):
        def body(q, carry):
            for u in range(8):
                b = q * 8 + u
                at = pl.ds(pl.multiple_of(b * 8, 8), 8)
                n = b if own else b + NB
                x1, x2, x3 = pieces(near_x[at, :])
                feat[n] = jnp.concatenate([x1, x2, x3, x1, x2, x1], 0).astype(BF16)
                c1, c2, c3 = pieces(tab_c[b] if own else halo_c[at, :])
                car[n] = jnp.concatenate([c1, c2, c3, jnp.zeros_like(c1)], 0).astype(BF16)
                if own:
                    p1, p2, p3 = pieces(tab_p[at, :])
                    own_feat[b] = jnp.concatenate([p1, p1, p1, p2, p2, p3], 0).astype(BF16)
            return carry

        lax.fori_loop(first // 8, last // 8, body, 0)

    features(st, True, 0, NB)
    convert(True, 0, NB)
    feat[NC] = jnp.zeros((FR, 128), BF16)
    car[NC] = jnp.zeros((CR, 128), BF16)

    mv = movers[...]
    per = mv.shape[0]
    live = lax.broadcasted_iota(jnp.int32, mv.shape, 0) < mover_counts[...]
    block_of = jnp.where(live, lax.shift_right_logical(mv, 7), -1)
    lane_of = mv & 127
    gone = jnp.zeros((NB, 128), F32)
    for r in range(0, per, 2):
        b = jnp.concatenate([block_of[r : r + 1], block_of[r + 1 : r + 2]], 1)
        ln = jnp.concatenate([lane_of[r : r + 1], lane_of[r + 1 : r + 2]], 1)
        in_block = (lax.broadcasted_iota(jnp.int32, (NB, 128), 0) == b).astype(F32).astype(BF16)
        in_lane = (lax.broadcasted_iota(jnp.int32, (128, 128), 0) == ln).astype(F32).astype(BF16)
        gone = gone + lax.dot_general(in_block, in_lane, NT, preferred_element_type=F32)
    stay[...] = 1.0 - gone

    for p in range(4):

        @pl.when(has[p])
        def _(p=p):
            for copy in copies(p ^ 1):
                copy.wait_recv()

        features(halo_x, False, p * HB, p * HB + HB)
        convert(False, p * HB, p * HB + HB)

    for p in range(4):

        @pl.when(has[p])
        def _(p=p):
            for copy in copies(p):
                copy.wait_send()


def exchange(lists, counts, planes, movers, mover_counts):
    smem, vmem = pl.BlockSpec(memory_space=pltpu.SMEM), pl.BlockSpec(memory_space=pltpu.VMEM)
    return pl.pallas_call(
        exchange_kernel,
        out_shape=(
            pltpu.VMEM((3, 4 * HB, 128), F32),
            pltpu.VMEM((NC + 1, FR, 128), BF16),
            pltpu.VMEM((NB, FR, 128), BF16),
            pltpu.VMEM((NC + 1, CR, 128), BF16),
            pltpu.VMEM((NB, 128), F32),
            pltpu.VMEM((12, NB, 128), F32),
        ),
        in_specs=[smem, smem, pl.BlockSpec(memory_space=pl.ANY), vmem, vmem],
        out_specs=(vmem,) * 6,
        scratch_shapes=[
            pltpu.VMEM((4 * HB * 8, 128), F32),
            pltpu.VMEM((NB, 8, 128), F32),
            pltpu.VMEM((NB, 8, 128), F32),
            pltpu.VMEM((NB * 8, 128), F32),
            pltpu.VMEM((NB * 8, 128), F32),
            pltpu.VMEM((4 * HB * 8, 128), F32),
            pltpu.VMEM((HB * 8, 128), F32),
            pltpu.VMEM((3, 4, HB, 128), F32),
            pltpu.SemaphoreType.DMA((4, 2)),
            pltpu.SemaphoreType.DMA((4, 2)),
            pltpu.SemaphoreType.DMA((LOADS,)),
        ],
        compiler_params=pltpu.CompilerParams(
            collective_id=0, has_side_effects=True, vmem_limit_bytes=VMEM_LIMIT
        ),
    )(lists, counts, planes, movers, mover_counts)


def swap_groups(v):
    row = lax.broadcasted_iota(jnp.int32, (8, 128), 0)
    group = lax.broadcasted_iota(jnp.int32, (8, 128), 1) // 16
    apart = (row - group) & 7
    out = v
    for d in range(1, 8):
        moved = pltpu.roll(pltpu.roll(v, d, 0), 128 - 16 * d, 1)
        out = jnp.where(apart == d, moved, out)
    return out


def local_kernel(
    nbr, mask, st, halo_x, feat, own_feat, car, stay_ref, kept_out, upd,
    tab_x, sums, kept, out_sem, *stages,
):
    dist, parts = stages[:RB], stages[RB:]
    wide = None
    for c in range(3):
        half = 0.5 * jnp.max(st[c]) - 0.5 * jnp.min(st[c])
        wide = half if wide is None else jnp.maximum(wide, half)
    close = wide <= REACH

    def slot(k, i):
        return jnp.where(mask[k, i] == 0, NC, nbr[k, i])

    def measure(p, u):
        one, two = 2 * p, 2 * p + 1
        mine = beside(own_feat[one], own_feat[two])
        for k in range(4):
            near = jnp.concatenate([feat[slot(k, one)], feat[slot(k, two)]], 0)
            dist[u][k * 128 : k * 128 + 128, :] = lax.dot_general(
                near, mine, TN, preferred_element_type=F32
            )

    def weigh(u):
        for n in range(2):
            for k in range(4):
                weights(dist[u], n * 128, k * 128, parts[u], (n * 4 + k) * 128)

    def contract(p, u):
        c = beside(*[
            jnp.concatenate([car[slot(k, i)] for k in range(4)], 1) for i in (2 * p, 2 * p + 1)
        ])
        r = jnp.dot(c, parts[u][...], preferred_element_type=F32)
        at = pl.multiple_of(p * 16, 16)
        sums[pl.ds(at, 8), :] = fold(r[0:CR])
        sums[pl.ds(at + 8, 8), :] = fold(r[CR:])

    @pl.when(close)
    def _():
        def body(t, carry):
            for u in range(U):
                p = t * U + u
                contract(jnp.maximum(p - 2, 0), (u - 2) % RB)
                weigh((u - 1) % RB)
                measure(p, u % RB)
            return carry

        lax.fori_loop(0, NB // 2 // U, body, 0)
        contract(NB // 2 - 2, RB - 2)
        weigh(RB - 1)
        contract(NB // 2 - 1, RB - 1)

    @pl.when(jnp.logical_not(close))
    def _():
        def raw(q, carry):
            own = pl.ds(pl.multiple_of(q * 32, 32), 32)
            for c in range(3):
                tab_x[pl.ds(q * 256 + c, 32, stride=8), :] = st[c, own, :]
                tab_x[pl.ds(NB * 8 + q * 256 + c, 32, stride=8), :] = halo_x[c, own, :]
            return carry

        lax.fori_loop(0, NB // 32, raw, 0)

        def body(i, carry):
            columns = jnp.transpose(tab_x[pl.ds(pl.multiple_of(i * 8, 8), 8), :])

            def pair(k, total):
                near = tab_x[pl.ds(pl.multiple_of(nbr[k, i] * 8, 8), 8), :]
                s = jnp.full((128, 128), 0.5, F32)
                for c in range(3):
                    delta = columns[:, c : c + 1] - near[c : c + 1, :]
                    s = s - delta * delta
                s = jnp.maximum(s, 0.0)
                h, rest = split(s * s * s)
                cc = car[slot(k, i)]
                return total + lax.dot_general(cc, jnp.concatenate([h, rest], 0), NT, preferred_element_type=F32)

            total = lax.fori_loop(0, 4, pair, jnp.zeros((CR, 256), F32))
            sums[pl.ds(pl.multiple_of(i * 8, 8), 8), :] = fold(total)
            return carry

        lax.fori_loop(0, NB, body, 0)

    def advance(q, carry):
        rows = pl.ds(pl.multiple_of(q * 32, 32), 32)
        total = [8.0 * sums[pl.ds(q * 256 + c, 32, stride=8), :] for c in range(8)]
        position = [st[c, rows, :] for c in range(3)]
        velocity = [st[3 + c, rows, :] for c in range(3)]
        temper, one, two, solid = (st[c, rows, :] for c in range(8, 12))
        vol = total[1]
        temp_one = temper + 0.25 * (total[2] - temper * vol)
        conc_one = one + 0.2 * (total[3] - one * vol)
        conc_two = two + 0.1 * (total[4] - two * vol)
        v_new = [velocity[c] + 0.3 * (total[5 + c] - velocity[c] * vol) for c in range(3)]
        x_new = [position[c] + 0.02 * v_new[c] for c in range(3)]
        liquidus = 1.0 - 0.3 * conc_one - 0.2 * conc_two
        solid_new = jnp.maximum(solid, jnp.clip(2.0 * (liquidus - temp_one), 0.0, 1.0))
        temp_two = temp_one + 0.4 * (solid_new - solid)
        one_new = conc_one * (1.0 - 0.83 * solid) / (1.0 - 0.83 * solid_new)
        two_new = conc_two * (1.0 - 0.6 * solid) / (1.0 - 0.6 * solid_new)
        updated = [*x_new, *v_new, st[6, rows, :], total[0], temp_two, one_new, two_new, solid_new]
        stay = stay_ref[rows, :]
        for c, plane in enumerate(updated):
            kept[c, rows, :] = plane * stay
            upd[rows, c, :] = plane
        zero = jnp.zeros((32, 128), F32)
        for c in range(12, 16):
            upd[rows, c, :] = zero
        leave(q).start()
        return carry

    def leave(q):
        rows = pl.ds(pl.multiple_of(q * 32, 32), 32)
        return pltpu.make_async_copy(kept.at[:, rows], kept_out.at[:, rows], out_sem.at[q])

    lax.fori_loop(0, NB // 32, advance, 0)
    for q in range(NB // 32):
        leave(q).wait()


def local_step(nbr, mask, planes, tables):
    smem, vmem = pl.BlockSpec(memory_space=pltpu.SMEM), pl.BlockSpec(memory_space=pltpu.VMEM)
    return pl.pallas_call(
        local_kernel,
        out_shape=(
            pltpu.HBM((12, NB, 128), F32),
            pltpu.VMEM((NB, 16, 128), F32),
        ),
        in_specs=[smem] * 2 + [vmem] * 6,
        out_specs=(pl.BlockSpec(memory_space=pl.ANY), vmem),
        scratch_shapes=[
            pltpu.VMEM((NC * 8, 128), F32),
            pltpu.VMEM((NB * 8, 128), F32),
            pltpu.VMEM((12, NB, 128), F32),
            pltpu.SemaphoreType.DMA((NB // 32,)),
            *[pltpu.VMEM((512, 256), F32)] * RB,
            *[pltpu.VMEM((1024, 256), BF16)] * RB,
        ],
        compiler_params=pltpu.CompilerParams(vmem_limit_bytes=VMEM_LIMIT),
    )(nbr, mask, pltpu.with_memory_space_constraint(planes, pltpu.VMEM), *[pltpu.with_memory_space_constraint(t, pltpu.VMEM) for t in tables])


def migrate_kernel(movers_s, counts_s, upd, out, message, landed, ssem, rsem):
    grp, me = lax.axis_index("grp"), lax.axis_index("dom")
    doms = 64

    def device(k):
        return (grp, lax.rem(me + k, doms))

    barrier = pltpu.get_barrier_semaphore()
    for k in range(1, doms):
        pl.semaphore_signal(barrier, inc=1, device_id=device(k), device_id_type=MESH)

    lane = lax.broadcasted_iota(jnp.int32, (16, 128), 1)

    def gather(g, carry):
        count = jnp.zeros((16, 128), jnp.int32)
        for q in range(8):
            count = jnp.where(lax.shift_right_logical(lane, 4) == q, counts_s[0, g * 8 + q], count)
        acc = jnp.zeros((16, 128), F32)
        for t in range(128):
            m = movers_s[t % 16, g * 8 + t // 16]
            acc = jnp.where(lane == t, pltpu.roll(upd[lax.shift_right_logical(m, 7)], (t - m) & 127, 1), acc)
        acc = jnp.where((lane & 15) < count, acc, 0.0)
        for h in range(2):
            message[pl.ds(g * 8, 8), h, :] = swap_groups(acc[8 * h : 8 * h + 8])
        return carry

    lax.fori_loop(0, 8, gather, 0)
    landed[me] = message[me]
    pl.semaphore_wait(barrier, doms - 1)

    def copy(k):
        return pltpu.make_async_remote_copy(
            src_ref=message.at[lax.rem(me + k, doms)],
            dst_ref=landed.at[me],
            send_sem=ssem.at[k],
            recv_sem=rsem.at[k],
            device_id=device(k),
            device_id_type=MESH,
        )

    copies = [copy(k) for k in range(1, doms)]
    for c in copies:
        c.start()
    for c in copies:
        c.wait_recv()
    for g in range(doms // 8):
        for h in range(2):
            rows = 8 if h == 0 else 4
            v = swap_groups(landed[pl.ds(g * 8, 8), h, :])
            out[8 * h : 8 * h + rows, g * 128 : g * 128 + 128] = v[:rows]
    for c in copies:
        c.wait_send()


def migrate(movers, counts, upd):
    smem, vmem = pl.BlockSpec(memory_space=pltpu.SMEM), pl.BlockSpec(memory_space=pltpu.VMEM)
    return pl.pallas_call(
        migrate_kernel,
        out_shape=jax.ShapeDtypeStruct((12, 1024), F32),
        in_specs=[smem, smem, vmem],
        out_specs=vmem,
        scratch_shapes=[
            pltpu.VMEM((64, 2, 128), F32),
            pltpu.VMEM((64, 2, 128), F32),
            pltpu.SemaphoreType.DMA((64,)),
            pltpu.SemaphoreType.DMA((64,)),
        ],
        compiler_params=pltpu.CompilerParams(
            collective_id=1, has_side_effects=True, vmem_limit_bytes=VMEM_LIMIT
        ),
    )(movers, counts, pltpu.with_memory_space_constraint(upd, pltpu.VMEM))


def on_device(state, neighbours, pair_mask, send_lists, send_counts, movers, mover_counts):
    def far(x):
        return pltpu.with_memory_space_constraint(x, pltpu.HBM)

    planes = far(state.transpose(1, 0, 2))
    slots, counts = far(movers[0].T), far(mover_counts)
    *tables, planes = exchange(far(send_lists[0]), far(send_counts), planes, slots, counts)
    kept, upd = local_step(far(neighbours.T), far(pair_mask.T), planes, tables)
    arrivals = migrate(slots, counts, upd)
    return kept.transpose(1, 0, 2), arrivals


def solution(mesh):
    both = ("grp", "dom")
    placed = (P(both, None, None), P(both, None), P(both, None), P(both, None, None), P(both, None), P(both, None, None), P(both, None))
    return jax.shard_map(
        on_device,
        mesh=mesh,
        in_specs=placed,
        out_specs=(P(both, None, None), P(None, both)),
        check_vma=False,
    )
```

```python
import jax
import jax.numpy as jnp
from jax import lax
from jax.experimental import pallas as pl
from jax.experimental.pallas import tpu as pltpu
from jax.sharding import PartitionSpec as P

MESH = pl.DeviceIdType.MESH
F32 = jnp.float32
BF16 = jnp.bfloat16
NB = 256
HB = 64
NC = 512
FR = 48
CR = 32
U = 64
RB = 4
LOADS = 4
REACH = 2.0
NT = (((1,), (1,)), ((), ()))
TN = (((0,), (0,)), ((), ()))
VMEM_LIMIT = 40 << 20


def carried_planes(st, rows):
    mass = st[6, rows, :]
    volume = mass / st[7, rows, :]
    out = [mass, volume]
    for ch in (8, 9, 10, 3, 4, 5):
        out.append(volume * st[ch, rows, :])
    return out


def split(w):
    h = w.astype(BF16)
    return h, (w - h.astype(F32)).astype(BF16)


def weights(dist, lane, row, parts, out_row):
    s = jnp.maximum(dist[row : row + 128, lane : lane + 128], 0.0)
    h, rest = split(s * s * s)
    parts[out_row : out_row + 128, 0:128] = h
    parts[out_row : out_row + 128, 128:256] = rest


def beside(one, two):
    return jnp.concatenate(
        [
            jnp.concatenate([one, jnp.zeros_like(two)], 1),
            jnp.concatenate([jnp.zeros_like(one), two], 1),
        ],
        0,
    )


def fold(r):
    r = r[:, 0:128] + r[:, 128:256]
    return r[0:8] + r[8:16] + r[16:24]


def pieces(v):
    first = v.astype(BF16).astype(F32)
    rest = v - first
    second = rest.astype(BF16).astype(F32)
    return first, second, rest - second


def exchange_kernel(
    lists, counts, state, movers, mover_counts, halo_x, feat, own_feat, car, stay, st,
    halo_c, tab_c, tab_x, near_x, tab_p, send_c, pick_x, send_x, ssem, rsem, load_sem,
):
    grp, dom = lax.axis_index("grp"), lax.axis_index("dom")
    n_grp, n_dom = lax.axis_size("grp"), lax.axis_size("dom")
    has = [dom > 0, dom < n_dom - 1, grp > 0, grp < n_grp - 1]
    peer = [(grp, dom - 1), (grp, dom + 1), (grp - 1, dom), (grp + 1, dom)]
    chunk = NB // LOADS
    loads = [
        pltpu.make_async_copy(
            state.at[:, pl.ds(q * chunk, chunk)], st.at[:, pl.ds(q * chunk, chunk)], load_sem.at[q]
        )
        for q in range(LOADS)
    ]
    for load in loads:
        load.start()
    barrier = pltpu.get_barrier_semaphore()
    for p in range(4):

        @pl.when(has[p])
        def _(p=p):
            pl.semaphore_signal(barrier, inc=1, device_id=peer[p], device_id_type=MESH)

    def build(q, carry):
        rows = pl.ds(pl.multiple_of(q * 32, 32), 32)
        for c, plane in enumerate(carried_planes(st, rows)):
            tab_c[rows, c, :] = plane
        for c in range(3):
            tab_x[rows, c, :] = st[c, rows, :]
        return carry

    for q, load in enumerate(loads):
        load.wait()
        lax.fori_loop(q * chunk // 32, (q + 1) * chunk // 32, build, 0)

    def copies(p):
        slot = p ^ 1
        return [
            pltpu.make_async_remote_copy(
                src_ref=send_c.at[pl.ds(p * HB * 8, HB * 8)],
                dst_ref=halo_c.at[pl.ds(slot * HB * 8, HB * 8)],
                send_sem=ssem.at[p, 0],
                recv_sem=rsem.at[slot, 0],
                device_id=peer[p],
                device_id_type=MESH,
            ),
            pltpu.make_async_remote_copy(
                src_ref=send_x.at[:, p],
                dst_ref=halo_x.at[:, pl.ds(slot * HB, HB)],
                send_sem=ssem.at[p, 1],
                recv_sem=rsem.at[slot, 1],
                device_id=peer[p],
                device_id_type=MESH,
            ),
        ]

    met = False
    for p in (3, 2, 1, 0):

        def pick(t, carry, p=p):
            for u in range(8):
                s = t * 8 + u
                live = jnp.where(s < counts[0, p], 1.0, 0.0).astype(F32)
                b = lists[p, s]
                send_c[pl.ds(pl.multiple_of(p * HB * 8 + s * 8, 8), 8), :] = tab_c[b] * live
                pick_x[pl.ds(pl.multiple_of(s * 8, 8), 8), :] = tab_x[b] * live
            return carry

        lax.fori_loop(0, HB // 8, pick, 0)
        for c in range(3):
            send_x[c, p] = pick_x[pl.ds(c, HB, stride=8), :]
        if not met:
            pl.semaphore_wait(barrier, sum(h.astype(jnp.int32) for h in has))
            met = True

        @pl.when(has[p])
        def _(p=p):
            for copy in copies(p):
                copy.start()

    for p in range(4):

        @pl.when(jnp.logical_not(has[p]))
        def _(p=p):
            halo_c[pl.ds(p * HB * 8, HB * 8), :] = jnp.zeros((HB * 8, 128), F32)
            halo_x[:, pl.ds(p * HB, HB), :] = jnp.zeros((3, HB, 128), F32)

    centre = [0.5 * jnp.max(st[c]) + 0.5 * jnp.min(st[c]) for c in range(3)]

    def features(source, own, first, last):
        def body(q, carry):
            rows = pl.ds(pl.multiple_of(q * 32, 32), 32)
            zero, one = jnp.zeros((32, 128), F32), jnp.ones((32, 128), F32)
            norm, xs = None, []
            for c in range(3):
                x = jnp.clip(source[c, rows, :] - centre[c], -REACH - 1.0, REACH + 1.0)
                norm = x * x if norm is None else norm + x * x
                xs.append(x)
            for c, plane in enumerate([*xs, 0.5 - norm, one, zero, zero, zero]):
                near_x[pl.ds(q * 256 + c, 32, stride=8), :] = plane
            if own:
                for c, plane in enumerate([*[2.0 * x for x in xs], one, -norm, zero, zero, zero]):
                    tab_p[pl.ds(q * 256 + c, 32, stride=8), :] = plane
            return carry

        lax.fori_loop(first // 32, last // 32, body, 0)

    def convert(own, first, last):
        def body(q, carry):
            for u in range(8):
                b = q * 8 + u
                at = pl.ds(pl.multiple_of(b * 8, 8), 8)
                n = b if own else b + NB
                x1, x2, x3 = pieces(near_x[at, :])
                feat[n] = jnp.concatenate([x1, x2, x3, x1, x2, x1], 0).astype(BF16)
                c1, c2, c3 = pieces(tab_c[b] if own else halo_c[at, :])
                car[n] = jnp.concatenate([c1, c2, c3, jnp.zeros_like(c1)], 0).astype(BF16)
                if own:
                    p1, p2, p3 = pieces(tab_p[at, :])
                    own_feat[b] = jnp.concatenate([p1, p1, p1, p2, p2, p3], 0).astype(BF16)
            return carry

        lax.fori_loop(first // 8, last // 8, body, 0)

    features(st, True, 0, NB)
    convert(True, 0, NB)
    feat[NC] = jnp.zeros((FR, 128), BF16)
    car[NC] = jnp.zeros((CR, 128), BF16)

    mv = movers[...]
    per = mv.shape[0]
    live = lax.broadcasted_iota(jnp.int32, mv.shape, 0) < mover_counts[...]
    block_of = jnp.where(live, lax.shift_right_logical(mv, 7), -1)
    lane_of = mv & 127
    gone = jnp.zeros((NB, 128), F32)
    for r in range(0, per, 2):
        b = jnp.concatenate([block_of[r : r + 1], block_of[r + 1 : r + 2]], 1)
        ln = jnp.concatenate([lane_of[r : r + 1], lane_of[r + 1 : r + 2]], 1)
        in_block = (lax.broadcasted_iota(jnp.int32, (NB, 128), 0) == b).astype(F32).astype(BF16)
        in_lane = (lax.broadcasted_iota(jnp.int32, (128, 128), 0) == ln).astype(F32).astype(BF16)
        gone = gone + lax.dot_general(in_block, in_lane, NT, preferred_element_type=F32)
    stay[...] = 1.0 - gone

    for p in range(4):

        @pl.when(has[p])
        def _(p=p):
            for copy in copies(p ^ 1):
                copy.wait_recv()

        features(halo_x, False, p * HB, p * HB + HB)
        convert(False, p * HB, p * HB + HB)

    for p in range(4):

        @pl.when(has[p])
        def _(p=p):
            for copy in copies(p):
                copy.wait_send()


def exchange(lists, counts, planes, movers, mover_counts):
    smem, vmem = pl.BlockSpec(memory_space=pltpu.SMEM), pl.BlockSpec(memory_space=pltpu.VMEM)
    return pl.pallas_call(
        exchange_kernel,
        out_shape=(
            pltpu.VMEM((3, 4 * HB, 128), F32),
            pltpu.VMEM((NC + 1, FR, 128), BF16),
            pltpu.VMEM((NB, FR, 128), BF16),
            pltpu.VMEM((NC + 1, CR, 128), BF16),
            pltpu.VMEM((NB, 128), F32),
            pltpu.VMEM((12, NB, 128), F32),
        ),
        in_specs=[smem, smem, pl.BlockSpec(memory_space=pl.ANY), vmem, vmem],
        out_specs=(vmem,) * 6,
        scratch_shapes=[
            pltpu.VMEM((4 * HB * 8, 128), F32),
            pltpu.VMEM((NB, 8, 128), F32),
            pltpu.VMEM((NB, 8, 128), F32),
            pltpu.VMEM((NB * 8, 128), F32),
            pltpu.VMEM((NB * 8, 128), F32),
            pltpu.VMEM((4 * HB * 8, 128), F32),
            pltpu.VMEM((HB * 8, 128), F32),
            pltpu.VMEM((3, 4, HB, 128), F32),
            pltpu.SemaphoreType.DMA((4, 2)),
            pltpu.SemaphoreType.DMA((4, 2)),
            pltpu.SemaphoreType.DMA((LOADS,)),
        ],
        compiler_params=pltpu.CompilerParams(
            collective_id=0, has_side_effects=True, vmem_limit_bytes=VMEM_LIMIT
        ),
    )(lists, counts, planes, movers, mover_counts)


def swap_groups(v):
    row = lax.broadcasted_iota(jnp.int32, (8, 128), 0)
    group = lax.broadcasted_iota(jnp.int32, (8, 128), 1) // 16
    apart = (row - group) & 7
    out = v
    for d in range(1, 8):
        moved = pltpu.roll(pltpu.roll(v, d, 0), 128 - 16 * d, 1)
        out = jnp.where(apart == d, moved, out)
    return out


def local_kernel(
    nbr, mask, st, halo_x, feat, own_feat, car, stay_ref, kept_out, upd,
    tab_x, sums, kept, out_sem, *stages,
):
    dist, parts = stages[:RB], stages[RB:]
    wide = None
    for c in range(3):
        half = 0.5 * jnp.max(st[c]) - 0.5 * jnp.min(st[c])
        wide = half if wide is None else jnp.maximum(wide, half)
    close = wide <= REACH

    def slot(k, i):
        return jnp.where(mask[k, i] == 0, NC, nbr[k, i])

    def measure(p, u):
        one, two = 2 * p, 2 * p + 1
        mine = beside(own_feat[one], own_feat[two])
        for k in range(4):
            near = jnp.concatenate([feat[slot(k, one)], feat[slot(k, two)]], 0)
            dist[u][k * 128 : k * 128 + 128, :] = lax.dot_general(
                near, mine, TN, preferred_element_type=F32
            )

    def weigh(u):
        for n in range(2):
            for k in range(4):
                weights(dist[u], n * 128, k * 128, parts[u], (n * 4 + k) * 128)

    def contract(p, u):
        c = beside(*[
            jnp.concatenate([car[slot(k, i)] for k in range(4)], 1) for i in (2 * p, 2 * p + 1)
        ])
        r = jnp.dot(c, parts[u][...], preferred_element_type=F32)
        at = pl.multiple_of(p * 16, 16)
        sums[pl.ds(at, 8), :] = fold(r[0:CR])
        sums[pl.ds(at + 8, 8), :] = fold(r[CR:])

    @pl.when(close)
    def _():
        def body(t, carry):
            for u in range(U):
                p = t * U + u
                contract(jnp.maximum(p - 2, 0), (u - 2) % RB)
                weigh((u - 1) % RB)
                measure(p, u % RB)
            return carry

        lax.fori_loop(0, NB // 2 // U, body, 0)
        contract(NB // 2 - 2, RB - 2)
        weigh(RB - 1)
        contract(NB // 2 - 1, RB - 1)

    @pl.when(jnp.logical_not(close))
    def _():
        def raw(q, carry):
            own = pl.ds(pl.multiple_of(q * 32, 32), 32)
            for c in range(3):
                tab_x[pl.ds(q * 256 + c, 32, stride=8), :] = st[c, own, :]
                tab_x[pl.ds(NB * 8 + q * 256 + c, 32, stride=8), :] = halo_x[c, own, :]
            return carry

        lax.fori_loop(0, NB // 32, raw, 0)

        def body(i, carry):
            columns = jnp.transpose(tab_x[pl.ds(pl.multiple_of(i * 8, 8), 8), :])

            def pair(k, total):
                near = tab_x[pl.ds(pl.multiple_of(nbr[k, i] * 8, 8), 8), :]
                s = jnp.full((128, 128), 0.5, F32)
                for c in range(3):
                    delta = columns[:, c : c + 1] - near[c : c + 1, :]
                    s = s - delta * delta
                s = jnp.maximum(s, 0.0)
                h, rest = split(s * s * s)
                cc = car[slot(k, i)]
                return total + lax.dot_general(cc, jnp.concatenate([h, rest], 0), NT, preferred_element_type=F32)

            total = lax.fori_loop(0, 4, pair, jnp.zeros((CR, 256), F32))
            sums[pl.ds(pl.multiple_of(i * 8, 8), 8), :] = fold(total)
            return carry

        lax.fori_loop(0, NB, body, 0)

    def advance(q, carry):
        rows = pl.ds(pl.multiple_of(q * 32, 32), 32)
        total = [8.0 * sums[pl.ds(q * 256 + c, 32, stride=8), :] for c in range(8)]
        position = [st[c, rows, :] for c in range(3)]
        velocity = [st[3 + c, rows, :] for c in range(3)]
        temper, one, two, solid = (st[c, rows, :] for c in range(8, 12))
        vol = total[1]
        temp_one = temper + 0.25 * (total[2] - temper * vol)
        conc_one = one + 0.2 * (total[3] - one * vol)
        conc_two = two + 0.1 * (total[4] - two * vol)
        v_new = [velocity[c] + 0.3 * (total[5 + c] - velocity[c] * vol) for c in range(3)]
        x_new = [position[c] + 0.02 * v_new[c] for c in range(3)]
        liquidus = 1.0 - 0.3 * conc_one - 0.2 * conc_two
        solid_new = jnp.maximum(solid, jnp.clip(2.0 * (liquidus - temp_one), 0.0, 1.0))
        temp_two = temp_one + 0.4 * (solid_new - solid)
        one_new = conc_one * (1.0 - 0.83 * solid) / (1.0 - 0.83 * solid_new)
        two_new = conc_two * (1.0 - 0.6 * solid) / (1.0 - 0.6 * solid_new)
        updated = [*x_new, *v_new, st[6, rows, :], total[0], temp_two, one_new, two_new, solid_new]
        stay = stay_ref[rows, :]
        for c, plane in enumerate(updated):
            kept[c, rows, :] = plane * stay
            upd[rows, c, :] = plane
        zero = jnp.zeros((32, 128), F32)
        for c in range(12, 16):
            upd[rows, c, :] = zero
        leave(q).start()
        return carry

    def leave(q):
        rows = pl.ds(pl.multiple_of(q * 32, 32), 32)
        return pltpu.make_async_copy(kept.at[:, rows], kept_out.at[:, rows], out_sem.at[q])

    lax.fori_loop(0, NB // 32, advance, 0)
    for q in range(NB // 32):
        leave(q).wait()


def local_step(nbr, mask, planes, tables):
    smem, vmem = pl.BlockSpec(memory_space=pltpu.SMEM), pl.BlockSpec(memory_space=pltpu.VMEM)
    return pl.pallas_call(
        local_kernel,
        out_shape=(
            pltpu.HBM((12, NB, 128), F32),
            pltpu.VMEM((NB, 16, 128), F32),
        ),
        in_specs=[smem] * 2 + [vmem] * 6,
        out_specs=(pl.BlockSpec(memory_space=pl.ANY), vmem),
        scratch_shapes=[
            pltpu.VMEM((NC * 8, 128), F32),
            pltpu.VMEM((NB * 8, 128), F32),
            pltpu.VMEM((12, NB, 128), F32),
            pltpu.SemaphoreType.DMA((NB // 32,)),
            *[pltpu.VMEM((512, 256), F32)] * RB,
            *[pltpu.VMEM((1024, 256), BF16)] * RB,
        ],
        compiler_params=pltpu.CompilerParams(vmem_limit_bytes=VMEM_LIMIT),
    )(nbr, mask, pltpu.with_memory_space_constraint(planes, pltpu.VMEM), *[pltpu.with_memory_space_constraint(t, pltpu.VMEM) for t in tables])


def migrate_kernel(movers_s, counts_s, upd, out, message, first, landed, ssem, rsem):
    grp, me = lax.axis_index("grp"), lax.axis_index("dom")
    y, z, core = me // 16, lax.rem(me // 2, 8), lax.rem(me, 2)
    place = y * 2 + core

    def across(k):
        other = lax.rem(place + k, 8)
        return other // 2, z, lax.rem(other, 2)

    def along(k):
        return y, lax.rem(z + k, 8), core

    def device(at):
        return (grp, at[0] * 16 + at[1] * 2 + at[2])

    barrier = pltpu.get_barrier_semaphore()
    for k in range(1, 8):
        for at in (across(k), along(k)):
            pl.semaphore_signal(barrier, inc=1, device_id=device(at), device_id_type=MESH)

    lane = lax.broadcasted_iota(jnp.int32, (16, 128), 1)

    def gather(k, carry):
        g = lax.rem(place + k, 8)

        def to(z):
            return (g // 2) * 16 + 2 * z + g % 2

        count = jnp.zeros((16, 128), jnp.int32)
        for q in range(8):
            count = jnp.where(lax.shift_right_logical(lane, 4) == q, counts_s[0, to(q)], count)
        acc = jnp.zeros((16, 128), F32)
        for t in range(128):
            m = movers_s[t % 16, to(t // 16)]
            acc = jnp.where(lane == t, pltpu.roll(upd[lax.shift_right_logical(m, 7)], (t - m) & 127, 1), acc)
        acc = jnp.where((lane & 15) < count, acc, 0.0)
        for h in range(2):
            message[g, :, h, :] = swap_groups(acc[8 * h : 8 * h + 8])
        return carry

    lax.fori_loop(1, 8, gather, 0)
    pl.semaphore_wait(barrier, 14)

    def hop_one(k):
        at = across(k)
        return pltpu.make_async_remote_copy(
            src_ref=message.at[at[0] * 2 + at[2]],
            dst_ref=first.at[place],
            send_sem=ssem.at[0, k],
            recv_sem=rsem.at[0, k],
            device_id=device(at),
            device_id_type=MESH,
        )

    def hop_two(k):
        at = along(k)
        return pltpu.make_async_remote_copy(
            src_ref=first.at[:, at[1]],
            dst_ref=landed.at[z],
            send_sem=ssem.at[1, k],
            recv_sem=rsem.at[1, k],
            device_id=device(at),
            device_id_type=MESH,
        )

    one, two = [hop_one(k) for k in range(1, 8)], [hop_two(k) for k in range(1, 8)]
    for copy in one:
        copy.start()
    lax.fori_loop(0, 1, gather, 0)
    first[place] = message[place]
    for copy in one:
        copy.wait_recv()
    for copy in two:
        copy.start()
    landed[z] = first[:, z]
    for copy in one:
        copy.wait_send()
    for copy in two:
        copy.wait()
    for g in range(8):
        for h in range(2):
            v = landed[pl.ds((g % 2) * 4, 4), pl.ds((g // 2) * 2, 2), h, :].reshape(8, 128)
            rows = 8 if h == 0 else 4
            out[8 * h : 8 * h + rows, g * 128 : g * 128 + 128] = swap_groups(v)[:rows]


def migrate(movers, counts, upd):
    smem, vmem = pl.BlockSpec(memory_space=pltpu.SMEM), pl.BlockSpec(memory_space=pltpu.VMEM)
    return pl.pallas_call(
        migrate_kernel,
        out_shape=jax.ShapeDtypeStruct((12, 1024), F32),
        in_specs=[smem, smem, vmem],
        out_specs=vmem,
        scratch_shapes=[
            pltpu.VMEM((8, 8, 2, 128), F32),
            pltpu.VMEM((8, 8, 2, 128), F32),
            pltpu.VMEM((8, 8, 2, 128), F32),
            pltpu.SemaphoreType.DMA((2, 8)),
            pltpu.SemaphoreType.DMA((2, 8)),
        ],
        compiler_params=pltpu.CompilerParams(
            collective_id=1, has_side_effects=True, vmem_limit_bytes=VMEM_LIMIT
        ),
    )(movers, counts, pltpu.with_memory_space_constraint(upd, pltpu.VMEM))


def on_device(state, neighbours, pair_mask, send_lists, send_counts, movers, mover_counts):
    def far(x):
        return pltpu.with_memory_space_constraint(x, pltpu.HBM)

    planes = far(state.transpose(1, 0, 2))
    slots, counts = far(movers[0].T), far(mover_counts)
    *tables, planes = exchange(far(send_lists[0]), far(send_counts), planes, slots, counts)
    kept, upd = local_step(far(neighbours.T), far(pair_mask.T), planes, tables)
    arrivals = migrate(slots, counts, upd)
    return kept.transpose(1, 0, 2), arrivals


def solution(mesh):
    both = ("grp", "dom")
    placed = (P(both, None, None), P(both, None), P(both, None), P(both, None, None), P(both, None), P(both, None, None), P(both, None))
    return jax.shard_map(
        on_device,
        mesh=mesh,
        in_specs=placed,
        out_specs=(P(both, None, None), P(None, both)),
        check_vma=False,
    )
```
